32 devices in a mesh: row: 4 (over x, core), col: 8 (over z, y).
Axes of the slice: x: 2, y: 2, z: 4, core: 2. Of those that a mesh axis runs over, the one named last changes fastest.
Arguments:
- matrix: float32 [8192, 16384], P('row', 'col'), may hold values from -40 to 40
Outputs:
- r_rows: float32 [512, 16384], P(None, 'col')
- scaled_basis: float32 [8192, 512], P('row')
- trailing: float32 [8192, 16384], P('row', 'col')
The draws below stay inside these ranges and needn't reach their ends.
All inputs are finite; a program needn't handle non-finite values.
Results may differ from the reference program's by a relative error of at most 0.00013.
Values sent between devices are 32-bit elements; how exact they have to be, the bound alone decides.
A program may use at most 128 MiB of HBM per device.

```python
import math
import jax
import jax.numpy as jnp
from jax import lax

N = 16384
B = 256
PANELS = 2
M = 8192
N_COL = 8


def draw_matrix(key, part):
    key_entries = jax.random.fold_in(key, 11)
    key_rows = jax.random.fold_in(key, 12)
    key_cols = jax.random.fold_in(key, 13)
    key_shared = jax.random.fold_in(key, 14)
    groups = (N + B - 1) // B
    share = 0.35
    remainder = math.sqrt(1.0 - share * share)
    row_scale = jnp.exp(jax.random.uniform(key_rows, (M, 1), jnp.float32) * math.log(10.0))
    col_scale = jnp.exp(jax.random.uniform(key_cols, (1, N), jnp.float32) * math.log(10.0))
    shared = jax.random.normal(key_shared, (M, groups), jnp.float32)
    noise = jax.random.normal(key_entries, (M, N), jnp.float32)
    spread = jnp.repeat(shared, B, axis=1)[:, :N]
    entries = jnp.clip(share * spread + remainder * noise, -4.0, 4.0)
    return 0.1 * entries * row_scale * col_scale


def setup_inputs(seed: int = 0) -> dict:
    keys = jax.random.split(jax.random.key(seed), 2)
    matrix = draw_matrix(jax.random.fold_in(keys[1], 71), 0)
    return {"matrix": matrix}


def product(left, right):
    return jnp.dot(left, right, precision=lax.Precision.HIGHEST)

def reference(matrix):
    current = matrix
    block_cols = N // N_COL
    r_blocks = []
    basis_blocks = []
    for panel_index in range(PANELS):
        panel_cols = current[:, panel_index * block_cols:panel_index * block_cols + B]
        gram_matrix = product(panel_cols.T, panel_cols)
        lower_factor = jnp.linalg.cholesky(gram_matrix)
        orthonormal = jax.scipy.linalg.solve_triangular(lower_factor, panel_cols.T, lower=True).T
        coupling = product(orthonormal.T, current)
        current = current - product(orthonormal, coupling)
        r_blocks.append(coupling)
        basis_blocks.append(orthonormal * math.sqrt(M))
    return (jnp.concatenate(r_blocks, axis=0), jnp.concatenate(basis_blocks, axis=1), current)
```

```python
import functools
import math

import jax
import jax.numpy as jnp
from jax import lax
from jax.experimental import pallas as pl
from jax.experimental.pallas import tpu as pltpu
from jax.sharding import PartitionSpec as P

B = 256
PANELS = 2
LANES = 128
SUB = 8
PIECES = 8
CHUNKS = B // LANES
BLOCKS = PANELS * CHUNKS
WIDTH = PANELS * B
MESH = pl.DeviceIdType.MESH
F32 = jnp.float32
ROWS_ROWS = (((0,), (0,)), ((), ()))
ROWS_COLS = (((1,), (0,)), ((), ()))
COLS_COLS = (((1,), (1,)), ((), ()))


def exact_dot(left, right, dims):
    return lax.dot_general(
        left, right, dims, precision=lax.Precision.HIGHEST, preferred_element_type=F32
    )


def split(x):
    high = x.astype(jnp.bfloat16)
    return high, (x - high.astype(F32)).astype(jnp.bfloat16)


def split_dot(left, right, dims):
    dot = functools.partial(lax.dot_general, dimension_numbers=dims, preferred_element_type=F32)
    return dot(left[0], right[0]) + (dot(left[0], right[1]) + dot(left[1], right[0]))


def gather_kernel(n_row, n_col, a_ref, w_ref, z_ref, g_ref, zacc, gacc, zcore, gcore, zmine, gmine,
                  zx, gx, piece_recv, z_send, y_send, core_send, core_recv, x_send, x_recv,
                  back_send, back_recv):
    ny = 1
    while 4 * ny * ny <= n_col:
        ny *= 2
    nz = n_col // ny
    nx = n_row // 2
    row, col = lax.axis_index("row"), lax.axis_index("col")
    zz, yy = col // ny, lax.rem(col, ny)
    xx, core = row // 2, lax.rem(row, 2)
    mate = xx * 2 + 1 - core
    rows, cols = a_ref.shape
    depth = rows // PIECES
    half = cols // 2
    total = CHUNKS * PIECES

    def across_y(d):
        return zz * ny + lax.rem(yy + d, ny)

    def across_x(d):
        return lax.rem(xx + d, nx) * 2 + core

    barrier = pltpu.get_barrier_semaphore()
    greeted = 0
    for d in sorted({1, nz - 1}):
        pl.semaphore_signal(barrier, inc=1, device_id={"col": lax.rem(zz + d, nz) * ny + yy},
                            device_id_type=MESH)
        greeted += 1
    for d in range(1, ny):
        pl.semaphore_signal(barrier, inc=1, device_id={"col": across_y(d)}, device_id_type=MESH)
        greeted += 1
    for d in range(1, nx):
        pl.semaphore_signal(barrier, inc=1, device_id={"row": across_x(d)}, device_id_type=MESH)
        greeted += 1
    pl.semaphore_signal(barrier, inc=1, device_id={"row": mate}, device_id_type=MESH)
    greeted += 1
    pl.semaphore_wait(barrier, greeted)

    def piece(panel, t):
        return w_ref.at[panel * CHUNKS + t // PIECES, pl.ds(lax.rem(t, PIECES) * depth, depth), :]

    def z_copy(panel, t):
        place = piece(panel, t)
        return pltpu.make_async_remote_copy(
            src_ref=place, dst_ref=place, send_sem=z_send.at[t], recv_sem=piece_recv.at[panel, t],
            device_id={"col": col + ny}, device_id_type=MESH)

    def y_copy(panel, t, d):
        place = piece(panel, t)
        return pltpu.make_async_remote_copy(
            src_ref=place, dst_ref=place, send_sem=y_send.at[d - 1, t],
            recv_sem=piece_recv.at[panel, t],
            device_id={"col": across_y(d)}, device_id_type=MESH)

    def pass_on(panel, t):
        @pl.when(zz < nz - 1)
        def _():
            z_copy(panel, t).start()
        for d in range(1, ny):
            y_copy(panel, t, d).start()

    for panel in range(PANELS):
        @pl.when(col == panel)
        def _():
            for j in range(CHUNKS):
                w_ref[panel * CHUNKS + j] = a_ref[:, j * LANES:(j + 1) * LANES]

            def begin(t, carry):
                pass_on(panel, t)
                return carry
            lax.fori_loop(0, total, begin, 0)

    def relay(t):
        for panel in range(PANELS):
            @pl.when((yy == panel) & (zz > 0))
            def _():
                z_copy(panel, t).wait_recv()
                pass_on(panel, t)

    def arrive(t):
        for panel in range(PANELS):
            @pl.when(yy != panel)
            def _():
                y_copy(panel, t, 1).wait_recv()

    def rows_of(panel):
        return slice(panel * LANES, (panel + 1) * LANES)

    def gram_width(j):
        return (j + 1) * LANES

    def core_copies(j):
        other = 1 - core
        z_part = pl.ds(pl.multiple_of(other * half, half), half)
        g_part = pl.ds(pl.multiple_of(other * B, B), gram_width(j))
        return [
            pltpu.make_async_remote_copy(
                src_ref=gacc.at[j, :, g_part], dst_ref=gcore.at[j, :, pl.ds(0, gram_width(j))],
                send_sem=core_send.at[j, 0], recv_sem=core_recv.at[j, 0],
                device_id={"row": mate}, device_id_type=MESH),
            pltpu.make_async_remote_copy(
                src_ref=zacc.at[j, :, z_part], dst_ref=zcore.at[j],
                send_sem=core_send.at[j, 1], recv_sem=core_recv.at[j, 1],
                device_id={"row": mate}, device_id_type=MESH),
        ]

    def x_copies(j, part):
        found = []
        for d in range(1, nx):
            if part == 0:
                width = pl.ds(0, gram_width(j))
                source, target = gmine.at[j, :, width], gx.at[d - 1, j, :, width]
            else:
                source, target = zmine.at[j], zx.at[d - 1, j]
            found.append(pltpu.make_async_remote_copy(
                src_ref=source, dst_ref=target,
                send_sem=x_send.at[d - 1, j, part], recv_sem=x_recv.at[d - 1, j, part],
                device_id={"row": across_x(d)}, device_id_type=MESH))
        return found

    def back_copies(j, part):
        found = []
        for panel in range(PANELS):
            block = pl.ds(panel * B + j * LANES, LANES)
            if part == 0:
                place = g_ref.at[block, pl.ds(pl.multiple_of(core * B, B), gram_width(j))]
            else:
                place = z_ref.at[block, pl.ds(pl.multiple_of(core * half, half), half)]
            found.append(pltpu.make_async_remote_copy(
                src_ref=place, dst_ref=place,
                send_sem=back_send.at[j, part, panel], recv_sem=back_recv.at[j, part, panel],
                device_id={"row": mate}, device_id_type=MESH))
        return found

    def core_sum(j):
        z_part = pl.ds(pl.multiple_of(core * half, half), half)
        g_part = pl.ds(pl.multiple_of(core * B, B), gram_width(j))
        first, second = core_copies(j)
        first.wait_recv()
        gmine[j, :, 0:gram_width(j)] = gacc[j, :, g_part] + gcore[j, :, 0:gram_width(j)]
        for copy in x_copies(j, 0):
            copy.start()
        second.wait_recv()
        zmine[j] = zacc[j, :, z_part] + zcore[j]
        for copy in x_copies(j, 1):
            copy.start()

    def x_sum(j, part):
        for copy in x_copies(j, part):
            copy.wait_recv()
        if part == 0:
            summed = gmine[j, :, 0:gram_width(j)]
            for d in range(nx - 1):
                summed = summed + gx[d, j, :, 0:gram_width(j)]
            for panel in range(PANELS):
                g_ref[panel * B + j * LANES:panel * B + (j + 1) * LANES,
                      pl.ds(pl.multiple_of(core * B, B), gram_width(j))] = summed[rows_of(panel)]
        else:
            for panel in range(PANELS):
                summed = zmine[j, rows_of(panel)]
                for d in range(nx - 1):
                    summed = summed + zx[d, j, rows_of(panel)]
                z_ref[panel * B + j * LANES:panel * B + (j + 1) * LANES,
                      pl.ds(pl.multiple_of(core * half, half), half)] = summed
        for copy in back_copies(j, part):
            copy.start()

    zacc[...] = jnp.zeros_like(zacc)
    gacc[...] = jnp.zeros_like(gacc)
    g_ref[...] = jnp.zeros_like(g_ref)
    relay(0)
    for j in range(CHUNKS):
        def step(i, carry, j=j):
            t = j * PIECES + i

            @pl.when(t + 1 < total)
            def _():
                relay(t + 1)
            arrive(t)
            here = pl.ds(i * depth, depth)
            fresh = jnp.concatenate(
                [w_ref[panel * CHUNKS + j, here, :] for panel in range(PANELS)], axis=1)
            left = split(fresh)
            for k in range(0, cols, 512):
                right = split(a_ref[here, k:k + 512])
                zacc[j, :, k:k + 512] += split_dot(left, right, ROWS_ROWS)
            for q in range(j + 1):
                old = fresh if q == j else jnp.concatenate(
                    [w_ref[panel * CHUNKS + q, here, :] for panel in range(PANELS)], axis=1)
                gram = exact_dot(fresh, old, ROWS_ROWS)
                for panel in range(PANELS):
                    spot = panel * B + q * LANES
                    gacc[j, :, spot:spot + LANES] += gram[:, rows_of(panel)]
            if j > 0:
                @pl.when(i == 1)
                def _():
                    core_sum(j - 1)
            return carry
        lax.fori_loop(0, PIECES, step, 0)
        for copy in core_copies(j):
            copy.start()
    last = CHUNKS - 1
    core_sum(last)
    for j in range(last):
        x_sum(j, 0)
        x_sum(j, 1)
    x_sum(last, 0)
    x_sum(last, 1)

    def waits(t, carry):
        for panel in range(PANELS):
            @pl.when(yy == panel)
            def _():
                @pl.when(zz < nz - 1)
                def _():
                    z_copy(panel, t).wait_send()
                for d in range(1, ny):
                    y_copy(panel, t, d).wait_send()
        return carry
    lax.fori_loop(0, total, waits, 0)
    for j in range(CHUNKS):
        for copy in core_copies(j):
            copy.wait_send()
        for part in range(2):
            for copy in x_copies(j, part):
                copy.wait_send()
            for copy in back_copies(j, part):
                copy.wait_send()
    for j in range(CHUNKS):
        for part in range(2):
            for panel in range(PANELS):
                block = pl.ds(panel * B + j * LANES, LANES)
                if part == 0:
                    place = g_ref.at[block, pl.ds(pl.multiple_of((1 - core) * B, B), gram_width(j))]
                else:
                    place = z_ref.at[block, pl.ds(pl.multiple_of((1 - core) * half, half), half)]
                pltpu.make_async_remote_copy(
                    src_ref=place, dst_ref=place,
                    send_sem=back_send.at[j, part, panel], recv_sem=back_recv.at[j, part, panel],
                    device_id={"row": mate}, device_id_type=MESH).wait_recv()


def invert_factor(m_ref):
    lane = lax.broadcasted_iota(jnp.int32, (SUB, 2 * LANES), 1)
    sub = lax.broadcasted_iota(jnp.int32, (SUB, 2 * LANES), 0)
    for g in range(LANES // SUB):
        base = g * SUB
        strip = m_ref[base:base + SUB, :]
        for k in range(SUB - 1):
            ratio = strip[:, base + k:base + k + 1] / strip[k:k + 1, base + k:base + k + 1]
            strip = strip - jnp.where(sub > k, ratio, 0.0) * strip[k:k + 1, :]
        pivots = jnp.sum(jnp.where(lane == base + sub, strip, 0.0), axis=1, keepdims=True)
        strip = strip / jnp.sqrt(pivots)
        m_ref[base:base + SUB, :] = strip
        if base + SUB < LANES:
            ahead = jnp.where(lane[:, :LANES] >= base + SUB, strip[:, :LANES], 0.0)
            change = exact_dot(ahead, strip, ROWS_ROWS)
            m_ref[base + SUB:, :] -= change[base + SUB:, :]


def factor(g_ref, s_ref, m_ref):
    def tile(i, j):
        return g_ref[i * LANES:(i + 1) * LANES, j * LANES:(j + 1) * LANES]

    for i in range(BLOCKS):
        for j in range(BLOCKS):
            known = j % CHUNKS <= i % CHUNKS
            s_ref[i * LANES:(i + 1) * LANES, j * LANES:(j + 1) * LANES] = (
                tile(i, j) if known else tile(j, i).T)
    ident = (lax.broadcasted_iota(jnp.int32, (WIDTH, WIDTH), 0)
             == lax.broadcasted_iota(jnp.int32, (WIDTH, WIDTH), 1)).astype(F32)
    s_ref[:, WIDTH:] = ident
    for b in range(BLOCKS):
        here = slice(b * LANES, (b + 1) * LANES)
        m_ref[:, :LANES] = s_ref[here, here]
        m_ref[:, LANES:] = ident[:LANES, :LANES]
        invert_factor(m_ref)
        strip = exact_dot(m_ref[:, LANES:], s_ref[here, :], ROWS_COLS)
        s_ref[here, :] = strip
        if b + 1 < BLOCKS:
            below = slice((b + 1) * LANES, WIDTH)
            s_ref[below, :] -= exact_dot(strip[:, below], strip, ROWS_ROWS)


def update_kernel(scale, g_ref, z_ref, w_ref, a_ref, r_ref, q_ref, t_ref,
                  s_ref, m_ref, inv_high, inv_low, r_high, r_low):
    cols = a_ref.shape[1]

    @pl.when(pl.program_id(0) == 0)
    def _():
        factor(g_ref, s_ref, m_ref)
        inverse = split(s_ref[:, WIDTH:])
        inv_high[...] = inverse[0]
        inv_low[...] = inverse[1]
        for k in range(0, cols, 512):
            r = split_dot(inverse, split(z_ref[:, k:k + 512]), ROWS_COLS)
            r_ref[:, k:k + 512] = r
            high, low = split(r)
            r_high[:, k:k + 512] = high
            r_low[:, k:k + 512] = low

    w = jnp.concatenate([w_ref[i] for i in range(BLOCKS)], axis=1)
    q = split_dot(split(w), (inv_high[...], inv_low[...]), COLS_COLS)
    q_ref[...] = q * scale
    q = split(q)
    for k in range(0, cols, 512):
        r = r_high[:, k:k + 512], r_low[:, k:k + 512]
        t_ref[:, k:k + 512] = a_ref[:, k:k + 512] - split_dot(q, r, ROWS_COLS)


def on_device(n_row, n_col, matrix):
    rows, cols = matrix.shape
    nx = n_row // 2
    half = cols // 2
    vmem = pl.BlockSpec(memory_space=pltpu.VMEM)
    dma = pltpu.SemaphoreType.DMA
    total = CHUNKS * PIECES
    ny = 1
    while 4 * ny * ny <= n_col:
        ny *= 2
    stacked = PANELS * LANES
    w, z, g = pl.pallas_call(
        functools.partial(gather_kernel, n_row, n_col),
        out_shape=(
            jax.ShapeDtypeStruct((BLOCKS, rows, LANES), F32),
            jax.ShapeDtypeStruct((WIDTH, cols), F32),
            jax.ShapeDtypeStruct((WIDTH, WIDTH), F32),
        ),
        in_specs=[vmem],
        out_specs=(vmem, vmem, vmem),
        scratch_shapes=[
            pltpu.VMEM((CHUNKS, stacked, cols), F32),
            pltpu.VMEM((CHUNKS, stacked, WIDTH), F32),
            pltpu.VMEM((CHUNKS, stacked, half), F32),
            pltpu.VMEM((CHUNKS, stacked, B), F32),
            pltpu.VMEM((CHUNKS, stacked, half), F32),
            pltpu.VMEM((CHUNKS, stacked, B), F32),
            pltpu.VMEM((nx - 1, CHUNKS, stacked, half), F32),
            pltpu.VMEM((nx - 1, CHUNKS, stacked, B), F32),
            dma((PANELS, total)),
            dma((total,)),
            dma((ny - 1, total)),
            dma((CHUNKS, 2)),
            dma((CHUNKS, 2)),
            dma((nx - 1, CHUNKS, 2)),
            dma((nx - 1, CHUNKS, 2)),
            dma((CHUNKS, 2, PANELS)),
            dma((CHUNKS, 2, PANELS)),
        ],
        compiler_params=pltpu.CompilerParams(
            collective_id=0, has_side_effects=True, vmem_limit_bytes=60 * 1024 * 1024),
        name="gather_and_multiply",
    )(matrix)
    step = 256
    return pl.pallas_call(
        functools.partial(update_kernel, math.sqrt(rows * n_row)),
        grid=(rows // step,),
        out_shape=(
            jax.ShapeDtypeStruct((WIDTH, cols), F32),
            jax.ShapeDtypeStruct((rows, WIDTH), F32),
            jax.ShapeDtypeStruct((rows, cols), F32),
        ),
        in_specs=[
            vmem,
            vmem,
            pl.BlockSpec((BLOCKS, step, LANES), lambda i: (0, i, 0)),
            pl.BlockSpec((step, cols), lambda i: (i, 0)),
        ],
        out_specs=(
            pl.BlockSpec((WIDTH, cols), lambda i: (0, 0)),
            pl.BlockSpec((step, WIDTH), lambda i: (i, 0)),
            pl.BlockSpec((step, cols), lambda i: (i, 0)),
        ),
        scratch_shapes=[
            pltpu.VMEM((WIDTH, 2 * WIDTH), F32),
            pltpu.VMEM((LANES, 2 * LANES), F32),
            pltpu.VMEM((WIDTH, WIDTH), jnp.bfloat16),
            pltpu.VMEM((WIDTH, WIDTH), jnp.bfloat16),
            pltpu.VMEM((WIDTH, cols), jnp.bfloat16),
            pltpu.VMEM((WIDTH, cols), jnp.bfloat16),
        ],
        compiler_params=pltpu.CompilerParams(vmem_limit_bytes=60 * 1024 * 1024),
        name="factor_and_update",
    )(g, z, w, matrix)


def solution(mesh):
    sizes = mesh.shape
    placed = (P("row", "col"),)
    return jax.shard_map(
        functools.partial(on_device, sizes["row"], sizes["col"]),
        mesh=mesh,
        in_specs=placed,
        out_specs=(P(None, "col"), P("row", None), P("row", "col")),
        check_vma=False,
    )
```

```python
import functools
import math

import jax
import jax.numpy as jnp
from jax import lax
from jax.experimental import pallas as pl
from jax.experimental.pallas import tpu as pltpu
from jax.sharding import PartitionSpec as P

B = 256
PANELS = 2
LANES = 128
SUB = 8
PIECES = 16
GROUP = 2
CHUNKS = B // LANES
BLOCKS = PANELS * CHUNKS
WIDTH = PANELS * B
MESH = pl.DeviceIdType.MESH
F32 = jnp.float32
ROWS_ROWS = (((0,), (0,)), ((), ()))
ROWS_COLS = (((1,), (0,)), ((), ()))
COLS_COLS = (((1,), (1,)), ((), ()))


def exact_dot(left, right, dims):
    return lax.dot_general(
        left, right, dims, precision=lax.Precision.HIGHEST, preferred_element_type=F32
    )


def split(x):
    high = x.astype(jnp.bfloat16)
    return high, (x - high.astype(F32)).astype(jnp.bfloat16)


def split_dot(left, right, dims):
    dot = functools.partial(lax.dot_general, dimension_numbers=dims, preferred_element_type=F32)
    return dot(left[0], right[0]) + (dot(left[0], right[1]) + dot(left[1], right[0]))


def gather_kernel(n_row, n_col, a_ref, w_ref, z_ref, inv_ref, g_ref, s_ref, m_ref, zacc, gacc, zcore, gcore, zmine, gmine,
                  zx, gx, piece_recv, z_send, y_send, core_send, core_recv, x_send, x_recv,
                  back_send, back_recv):
    ny = 1
    while 4 * ny * ny <= n_col:
        ny *= 2
    nz = n_col // ny
    nx = n_row // 2
    row, col = lax.axis_index("row"), lax.axis_index("col")
    zz, yy = col // ny, lax.rem(col, ny)
    xx, core = row // 2, lax.rem(row, 2)
    mate = xx * 2 + 1 - core
    rows, cols = a_ref.shape
    depth = rows // PIECES
    half = cols // 2
    total = CHUNKS * PIECES

    def across_y(d):
        return zz * ny + lax.rem(yy + d, ny)

    def across_x(d):
        return lax.rem(xx + d, nx) * 2 + core

    barrier = pltpu.get_barrier_semaphore()
    greeted = 0
    for d in sorted({1, nz - 1}):
        pl.semaphore_signal(barrier, inc=1, device_id={"col": lax.rem(zz + d, nz) * ny + yy},
                            device_id_type=MESH)
        greeted += 1
    for d in range(1, ny):
        pl.semaphore_signal(barrier, inc=1, device_id={"col": across_y(d)}, device_id_type=MESH)
        greeted += 1
    for d in range(1, nx):
        pl.semaphore_signal(barrier, inc=1, device_id={"row": across_x(d)}, device_id_type=MESH)
        greeted += 1
    pl.semaphore_signal(barrier, inc=1, device_id={"row": mate}, device_id_type=MESH)
    greeted += 1
    pl.semaphore_wait(barrier, greeted)

    def piece(panel, t):
        return w_ref.at[panel * CHUNKS + t // PIECES, pl.ds(lax.rem(t, PIECES) * depth, depth), :]

    def z_copy(panel, t):
        place = piece(panel, t)
        return pltpu.make_async_remote_copy(
            src_ref=place, dst_ref=place, send_sem=z_send.at[t], recv_sem=piece_recv.at[panel, t],
            device_id={"col": col + ny}, device_id_type=MESH)

    def y_copy(panel, t, d):
        place = piece(panel, t)
        return pltpu.make_async_remote_copy(
            src_ref=place, dst_ref=place, send_sem=y_send.at[d - 1, t],
            recv_sem=piece_recv.at[panel, t],
            device_id={"col": across_y(d)}, device_id_type=MESH)

    def pass_on(panel, t):
        @pl.when(zz < nz - 1)
        def _():
            z_copy(panel, t).start()
        for d in range(1, ny):
            y_copy(panel, t, d).start()

    for panel in range(PANELS):
        @pl.when(col == panel)
        def _():
            for j in range(CHUNKS):
                w_ref[panel * CHUNKS + j] = a_ref[:, j * LANES:(j + 1) * LANES]

            def begin(t, carry):
                pass_on(panel, t)
                return carry
            lax.fori_loop(0, total, begin, 0)

    def relay(t):
        for panel in range(PANELS):
            @pl.when((yy == panel) & (zz > 0))
            def _():
                z_copy(panel, t).wait_recv()
                pass_on(panel, t)

    def arrive(t):
        for panel in range(PANELS):
            @pl.when(yy != panel)
            def _():
                y_copy(panel, t, 1).wait_recv()

    def rows_of(panel):
        return slice(panel * LANES, (panel + 1) * LANES)

    def gram_width(j):
        return (j + 1) * LANES

    def core_copies(j):
        other = 1 - core
        z_part = pl.ds(pl.multiple_of(other * half, half), half)
        g_part = pl.ds(pl.multiple_of(other * B, B), gram_width(j))
        return [
            pltpu.make_async_remote_copy(
                src_ref=gacc.at[j, :, g_part], dst_ref=gcore.at[j, :, pl.ds(0, gram_width(j))],
                send_sem=core_send.at[j, 0], recv_sem=core_recv.at[j, 0],
                device_id={"row": mate}, device_id_type=MESH),
            pltpu.make_async_remote_copy(
                src_ref=zacc.at[j, :, z_part], dst_ref=zcore.at[j],
                send_sem=core_send.at[j, 1], recv_sem=core_recv.at[j, 1],
                device_id={"row": mate}, device_id_type=MESH),
        ]

    def x_copies(j, part):
        found = []
        for d in range(1, nx):
            if part == 0:
                width = pl.ds(0, gram_width(j))
                source, target = gmine.at[j, :, width], gx.at[d - 1, j, :, width]
            else:
                source, target = zmine.at[j], zx.at[d - 1, j]
            found.append(pltpu.make_async_remote_copy(
                src_ref=source, dst_ref=target,
                send_sem=x_send.at[d - 1, j, part], recv_sem=x_recv.at[d - 1, j, part],
                device_id={"row": across_x(d)}, device_id_type=MESH))
        return found

    def back_copies(j, part):
        found = []
        for panel in range(PANELS):
            block = pl.ds(panel * B + j * LANES, LANES)
            if part == 0:
                place = g_ref.at[block, pl.ds(pl.multiple_of(core * B, B), gram_width(j))]
            else:
                place = z_ref.at[block, pl.ds(pl.multiple_of(core * half, half), half)]
            found.append(pltpu.make_async_remote_copy(
                src_ref=place, dst_ref=place,
                send_sem=back_send.at[j, part, panel], recv_sem=back_recv.at[j, part, panel],
                device_id={"row": mate}, device_id_type=MESH))
        return found

    def back_arrive(j, part):
        for panel in range(PANELS):
            block = pl.ds(panel * B + j * LANES, LANES)
            if part == 0:
                place = g_ref.at[block, pl.ds(pl.multiple_of((1 - core) * B, B), gram_width(j))]
            else:
                place = z_ref.at[block, pl.ds(pl.multiple_of((1 - core) * half, half), half)]
            pltpu.make_async_remote_copy(
                src_ref=place, dst_ref=place,
                send_sem=back_send.at[j, part, panel], recv_sem=back_recv.at[j, part, panel],
                device_id={"row": mate}, device_id_type=MESH).wait_recv()

    def core_sum(j):
        z_part = pl.ds(pl.multiple_of(core * half, half), half)
        g_part = pl.ds(pl.multiple_of(core * B, B), gram_width(j))
        first, second = core_copies(j)
        first.wait_recv()
        gmine[j, :, 0:gram_width(j)] = gacc[j, :, g_part] + gcore[j, :, 0:gram_width(j)]
        for copy in x_copies(j, 0):
            copy.start()
        second.wait_recv()
        zmine[j] = zacc[j, :, z_part] + zcore[j]
        for copy in x_copies(j, 1):
            copy.start()

    def x_sum(j, part):
        for copy in x_copies(j, part):
            copy.wait_recv()
        if part == 0:
            summed = gmine[j, :, 0:gram_width(j)]
            for d in range(nx - 1):
                summed = summed + gx[d, j, :, 0:gram_width(j)]
            for panel in range(PANELS):
                g_ref[panel * B + j * LANES:panel * B + (j + 1) * LANES,
                      pl.ds(pl.multiple_of(core * B, B), gram_width(j))] = summed[rows_of(panel)]
        else:
            for panel in range(PANELS):
                summed = zmine[j, rows_of(panel)]
                for d in range(nx - 1):
                    summed = summed + zx[d, j, rows_of(panel)]
                z_ref[panel * B + j * LANES:panel * B + (j + 1) * LANES,
                      pl.ds(pl.multiple_of(core * half, half), half)] = summed
        for copy in back_copies(j, part):
            copy.start()

    zacc[...] = jnp.zeros_like(zacc)
    gacc[...] = jnp.zeros_like(gacc)
    g_ref[...] = jnp.zeros_like(g_ref)
    for t in range(GROUP):
        relay(t)
    for j in range(CHUNKS):
        def step(i, carry, j=j):
            t = j * PIECES + GROUP * i
            here = pl.ds(i * GROUP * depth, GROUP * depth)
            for u in range(GROUP):
                arrive(t + u)
            fresh = jnp.concatenate(
                [w_ref[panel * CHUNKS + j, here, :] for panel in range(PANELS)], axis=1)
            left = split(fresh)
            span = cols // GROUP
            for u in range(GROUP):
                @pl.when(t + GROUP + u < total)
                def _():
                    relay(t + GROUP + u)
                for k in range(u * span, (u + 1) * span, 512):
                    right = split(a_ref[here, k:k + 512])
                    zacc[j, :, k:k + 512] += split_dot(left, right, ROWS_ROWS)
            for q in range(j + 1):
                old = fresh if q == j else jnp.concatenate(
                    [w_ref[panel * CHUNKS + q, here, :] for panel in range(PANELS)], axis=1)
                gram = exact_dot(fresh, old, ROWS_ROWS)
                for panel in range(PANELS):
                    spot = panel * B + q * LANES
                    gacc[j, :, spot:spot + LANES] += gram[:, rows_of(panel)]
            if j > 0:
                @pl.when(i == 1)
                def _():
                    core_sum(j - 1)
            return carry
        lax.fori_loop(0, PIECES // GROUP, step, 0)
        for copy in core_copies(j):
            copy.start()
    last = CHUNKS - 1
    core_sum(last)
    for j in range(CHUNKS):
        x_sum(j, 0)
    for j in range(CHUNKS):
        back_arrive(j, 0)
    for j in range(last):
        x_sum(j, 1)
    factor(g_ref, s_ref, m_ref)
    inv_ref[...] = s_ref[:, WIDTH:]
    x_sum(last, 1)

    def waits(t, carry):
        for panel in range(PANELS):
            @pl.when(yy == panel)
            def _():
                @pl.when(zz < nz - 1)
                def _():
                    z_copy(panel, t).wait_send()
                for d in range(1, ny):
                    y_copy(panel, t, d).wait_send()
        return carry
    lax.fori_loop(0, total, waits, 0)
    for j in range(CHUNKS):
        for copy in core_copies(j):
            copy.wait_send()
        for part in range(2):
            for copy in x_copies(j, part):
                copy.wait_send()
            for copy in back_copies(j, part):
                copy.wait_send()
    for j in range(CHUNKS):
        back_arrive(j, 1)


def invert_factor(m_ref):
    lane = lax.broadcasted_iota(jnp.int32, (SUB, LANES), 1)
    sub = lax.broadcasted_iota(jnp.int32, (SUB, LANES), 0)
    strip = m_ref[0:SUB, :]
    for g in range(LANES // SUB):
        base = g * SUB
        left, right = strip[:, :LANES], strip[:, LANES:]
        entry = {}
        for k in range(SUB):
            column = jnp.broadcast_to(left[:, base + k:base + k + 1], (SUB, LANES))
            for i in range(k, SUB):
                entry[i, k] = jnp.broadcast_to(column[i:i + 1, :], (SUB, LANES))
        low, inv = {}, {}
        for k in range(SUB):
            pivot = entry[k, k]
            guess = lax.rsqrt(pivot)
            guess = guess * (1.5 - (0.5 * pivot) * guess * guess)
            inv[k, k] = guess
            for i in range(k + 1, SUB):
                low[i, k] = entry[i, k] * guess
            for j in range(k + 1, SUB):
                for i in range(j, SUB):
                    entry[i, j] = entry[i, j] - low[i, k] * low[j, k]
        for i in range(SUB):
            for j in range(i):
                acc = low[i, j] * inv[j, j]
                for k in range(j + 1, i):
                    acc = acc + low[i, k] * inv[k, j]
                inv[i, j] = -acc * inv[i, i]
        done = []
        for side in (left, right):
            acc = None
            for j in range(SUB):
                weight = jnp.zeros((SUB, LANES), F32)
                for i in range(j, SUB):
                    weight = jnp.where(sub == i, inv[i, j], weight)
                term = weight * side[j:j + 1, :]
                acc = term if acc is None else acc + term
            done.append(acc)
        m_ref[base:base + SUB, :LANES] = done[0]
        m_ref[base:base + SUB, LANES:] = done[1]
        after = base + SUB
        if after < LANES:
            fresh = [m_ref[after:after + SUB, :LANES], m_ref[after:after + SUB, LANES:]]
            for i in range(SUB):
                column = jnp.broadcast_to(done[0][:, after + i:after + i + 1], (SUB, LANES))
                for side in range(2):
                    change = jnp.sum(column * done[side], axis=0, keepdims=True)
                    fresh[side] = jnp.where(sub == i, fresh[side] - change, fresh[side])
            strip = jnp.concatenate(fresh, axis=1)
        if after + SUB < LANES:
            ahead = jnp.where(lane >= after + SUB, done[0], 0.0)
            change = exact_dot(ahead, jnp.concatenate(done, axis=1), ROWS_ROWS)
            m_ref[after + SUB:, :] -= change[after + SUB:, :]


def factor(g_ref, s_ref, m_ref):
    def tile(i, j):
        return g_ref[i * LANES:(i + 1) * LANES, j * LANES:(j + 1) * LANES]

    for i in range(BLOCKS):
        for j in range(BLOCKS):
            known = j % CHUNKS <= i % CHUNKS
            s_ref[i * LANES:(i + 1) * LANES, j * LANES:(j + 1) * LANES] = (
                tile(i, j) if known else tile(j, i).T)
    ident = (lax.broadcasted_iota(jnp.int32, (WIDTH, WIDTH), 0)
             == lax.broadcasted_iota(jnp.int32, (WIDTH, WIDTH), 1)).astype(F32)
    s_ref[:, WIDTH:] = ident
    block_of = lax.broadcasted_iota(jnp.int32, (LANES, WIDTH), 1) // LANES

    def eliminate(b, carry):
        here = pl.ds(pl.multiple_of(b * LANES, LANES), LANES)
        m_ref[:, :LANES] = s_ref[here, here]
        m_ref[:, LANES:] = ident[:LANES, :LANES]
        invert_factor(m_ref)
        strip = exact_dot(m_ref[:, LANES:], s_ref[here, :], ROWS_COLS)
        s_ref[here, :] = strip

        @pl.when(b + 1 < BLOCKS)
        def _():
            ahead = jnp.where(block_of > b, strip[:, :WIDTH], 0.0)
            s_ref[...] -= exact_dot(ahead, strip, ROWS_ROWS)
        return carry
    lax.fori_loop(0, BLOCKS, eliminate, 0)


def update_kernel(scale, inv_ref, z_ref, w_ref, a_ref, r_ref, q_ref, t_ref,
                  inv_high, inv_low, r_high, r_low):
    cols = a_ref.shape[1]

    @pl.when(pl.program_id(0) == 0)
    def _():
        inverse = split(inv_ref[...])
        inv_high[...] = inverse[0]
        inv_low[...] = inverse[1]
        for k in range(0, cols, 512):
            r = split_dot(inverse, split(z_ref[:, k:k + 512]), ROWS_COLS)
            r_ref[:, k:k + 512] = r
            high, low = split(r)
            r_high[:, k:k + 512] = high
            r_low[:, k:k + 512] = low

    w = jnp.concatenate([w_ref[i] for i in range(BLOCKS)], axis=1)
    q = split_dot(split(w), (inv_high[...], inv_low[...]), COLS_COLS)
    q_ref[...] = q * scale
    q = split(q)
    for k in range(0, cols, 512):
        r = r_high[:, k:k + 512], r_low[:, k:k + 512]
        t_ref[:, k:k + 512] = a_ref[:, k:k + 512] - split_dot(q, r, ROWS_COLS)


def on_device(n_row, n_col, matrix):
    rows, cols = matrix.shape
    nx = n_row // 2
    half = cols // 2
    vmem = pl.BlockSpec(memory_space=pltpu.VMEM)
    dma = pltpu.SemaphoreType.DMA
    total = CHUNKS * PIECES
    ny = 1
    while 4 * ny * ny <= n_col:
        ny *= 2
    stacked = PANELS * LANES
    w, z, inverse = pl.pallas_call(
        functools.partial(gather_kernel, n_row, n_col),
        out_shape=(
            jax.ShapeDtypeStruct((BLOCKS, rows, LANES), F32),
            jax.ShapeDtypeStruct((WIDTH, cols), F32),
            jax.ShapeDtypeStruct((WIDTH, WIDTH), F32),
        ),
        in_specs=[vmem],
        out_specs=(vmem, vmem, vmem),
        scratch_shapes=[
            pltpu.VMEM((WIDTH, WIDTH), F32),
            pltpu.VMEM((WIDTH, 2 * WIDTH), F32),
            pltpu.VMEM((LANES, 2 * LANES), F32),
            pltpu.VMEM((CHUNKS, stacked, cols), F32),
            pltpu.VMEM((CHUNKS, stacked, WIDTH), F32),
            pltpu.VMEM((CHUNKS, stacked, half), F32),
            pltpu.VMEM((CHUNKS, stacked, B), F32),
            pltpu.VMEM((CHUNKS, stacked, half), F32),
            pltpu.VMEM((CHUNKS, stacked, B), F32),
            pltpu.VMEM((nx - 1, CHUNKS, stacked, half), F32),
            pltpu.VMEM((nx - 1, CHUNKS, stacked, B), F32),
            dma((PANELS, total)),
            dma((total,)),
            dma((ny - 1, total)),
            dma((CHUNKS, 2)),
            dma((CHUNKS, 2)),
            dma((nx - 1, CHUNKS, 2)),
            dma((nx - 1, CHUNKS, 2)),
            dma((CHUNKS, 2, PANELS)),
            dma((CHUNKS, 2, PANELS)),
        ],
        compiler_params=pltpu.CompilerParams(
            collective_id=0, has_side_effects=True, vmem_limit_bytes=60 * 1024 * 1024),
        name="gather_and_multiply",
    )(matrix)
    step = 256
    return pl.pallas_call(
        functools.partial(update_kernel, math.sqrt(rows * n_row)),
        grid=(rows // step,),
        out_shape=(
            jax.ShapeDtypeStruct((WIDTH, cols), F32),
            jax.ShapeDtypeStruct((rows, WIDTH), F32),
            jax.ShapeDtypeStruct((rows, cols), F32),
        ),
        in_specs=[
            vmem,
            vmem,
            pl.BlockSpec((BLOCKS, step, LANES), lambda i: (0, i, 0)),
            pl.BlockSpec((step, cols), lambda i: (i, 0)),
        ],
        out_specs=(
            pl.BlockSpec((WIDTH, cols), lambda i: (0, 0)),
            pl.BlockSpec((step, WIDTH), lambda i: (i, 0)),
            pl.BlockSpec((step, cols), lambda i: (i, 0)),
        ),
        scratch_shapes=[
            pltpu.VMEM((WIDTH, WIDTH), jnp.bfloat16),
            pltpu.VMEM((WIDTH, WIDTH), jnp.bfloat16),
            pltpu.VMEM((WIDTH, cols), jnp.bfloat16),
            pltpu.VMEM((WIDTH, cols), jnp.bfloat16),
        ],
        compiler_params=pltpu.CompilerParams(vmem_limit_bytes=60 * 1024 * 1024),
        name="factor_and_update",
    )(inverse, z, w, matrix)


def solution(mesh):
    sizes = mesh.shape
    placed = (P("row", "col"),)
    return jax.shard_map(
        functools.partial(on_device, sizes["row"], sizes["col"]),
        mesh=mesh,
        in_specs=placed,
        out_specs=(P(None, "col"), P("row", None), P("row", "col")),
        check_vma=False,
    )
```

```python
import functools
import math

import jax
import jax.numpy as jnp
from jax import lax
from jax.experimental import pallas as pl
from jax.experimental.pallas import tpu as pltpu
from jax.sharding import PartitionSpec as P

B = 256
PANELS = 2
LANES = 128
SUB = 8
PIECES = 16
GROUP = 2
AHEAD = 3
CHUNKS = B // LANES
BLOCKS = PANELS * CHUNKS
WIDTH = PANELS * B
MESH = pl.DeviceIdType.MESH
F32 = jnp.float32
ROWS_ROWS = (((0,), (0,)), ((), ()))
ROWS_COLS = (((1,), (0,)), ((), ()))
COLS_COLS = (((1,), (1,)), ((), ()))


def exact_dot(left, right, dims):
    return lax.dot_general(
        left, right, dims, precision=lax.Precision.HIGHEST, preferred_element_type=F32
    )


def split(x):
    high = x.astype(jnp.bfloat16)
    return high, (x - high.astype(F32)).astype(jnp.bfloat16)


def split_dot(left, right, dims):
    dot = functools.partial(lax.dot_general, dimension_numbers=dims, preferred_element_type=F32)
    return dot(left[0], right[0]) + (dot(left[0], right[1]) + dot(left[1], right[0]))


def gather_kernel(n_row, n_col, a_hbm, w_ref, z_ref, inv_ref, a_ref, a_sem, p_sem, g_ref, s_ref, m_ref, zacc, gacc, zcore, gcore, zmine, gmine,
                  zx, gx, piece_recv, z_send, y_send, core_send, core_recv, x_send, x_recv,
                  back_send, back_recv):
    ny = 1
    while 4 * ny * ny <= n_col:
        ny *= 2
    nz = n_col // ny
    nx = n_row // 2
    row, col = lax.axis_index("row"), lax.axis_index("col")
    zz, yy = col // ny, lax.rem(col, ny)
    xx, core = row // 2, lax.rem(row, 2)
    mate = xx * 2 + 1 - core
    rows, cols = a_hbm.shape
    depth = rows // PIECES
    half = cols // 2
    total = CHUNKS * PIECES

    def across_y(d):
        return zz * ny + lax.rem(yy + d, ny)

    def across_x(d):
        return lax.rem(xx + d, nx) * 2 + core

    def panel_copies(panel):
        return [pltpu.make_async_copy(a_hbm.at[:, pl.ds(j * LANES, LANES)],
                                      w_ref.at[panel * CHUNKS + j], p_sem.at[j])
                for j in range(CHUNKS)]

    for panel in range(PANELS):
        @pl.when(col == panel)
        def _():
            for copy in panel_copies(panel):
                copy.start()
    load = pltpu.make_async_copy(a_hbm, a_ref, a_sem)
    load.start()

    barrier = pltpu.get_barrier_semaphore()
    greeted = 0
    for d in sorted({1, nz - 1}):
        pl.semaphore_signal(barrier, inc=1, device_id={"col": lax.rem(zz + d, nz) * ny + yy},
                            device_id_type=MESH)
        greeted += 1
    for d in range(1, ny):
        pl.semaphore_signal(barrier, inc=1, device_id={"col": across_y(d)}, device_id_type=MESH)
        greeted += 1
    for d in range(1, nx):
        pl.semaphore_signal(barrier, inc=1, device_id={"row": across_x(d)}, device_id_type=MESH)
        greeted += 1
    pl.semaphore_signal(barrier, inc=1, device_id={"row": mate}, device_id_type=MESH)
    greeted += 1
    pl.semaphore_wait(barrier, greeted)

    def piece(panel, t):
        return w_ref.at[panel * CHUNKS + t // PIECES, pl.ds(lax.rem(t, PIECES) * depth, depth), :]

    def z_copy(panel, t):
        place = piece(panel, t)
        return pltpu.make_async_remote_copy(
            src_ref=place, dst_ref=place, send_sem=z_send.at[t], recv_sem=piece_recv.at[panel, t],
            device_id={"col": col + ny}, device_id_type=MESH)

    def y_copy(panel, t, d):
        place = piece(panel, t)
        return pltpu.make_async_remote_copy(
            src_ref=place, dst_ref=place, send_sem=y_send.at[d - 1, t],
            recv_sem=piece_recv.at[panel, t],
            device_id={"col": across_y(d)}, device_id_type=MESH)

    def pass_on(panel, t):
        @pl.when(zz < nz - 1)
        def _():
            z_copy(panel, t).start()
        for d in range(1, ny):
            y_copy(panel, t, d).start()

    for panel in range(PANELS):
        @pl.when(col == panel)
        def _():
            def begin(t, carry):
                pass_on(panel, t)
                return carry
            for j, copy in enumerate(panel_copies(panel)):
                copy.wait()
                lax.fori_loop(j * PIECES, (j + 1) * PIECES, begin, 0)

    def relay(t):
        for panel in range(PANELS):
            @pl.when((yy == panel) & (zz > 0))
            def _():
                z_copy(panel, t).wait_recv()
                pass_on(panel, t)

    def arrive(t):
        for panel in range(PANELS):
            @pl.when(yy != panel)
            def _():
                y_copy(panel, t, 1).wait_recv()

    def rows_of(panel):
        return slice(panel * LANES, (panel + 1) * LANES)

    def gram_width(j):
        return (j + 1) * LANES

    def core_copies(j):
        other = 1 - core
        z_part = pl.ds(pl.multiple_of(other * half, half), half)
        g_part = pl.ds(pl.multiple_of(other * B, B), gram_width(j))
        return [
            pltpu.make_async_remote_copy(
                src_ref=gacc.at[j, :, g_part], dst_ref=gcore.at[j, :, pl.ds(0, gram_width(j))],
                send_sem=core_send.at[j, 0], recv_sem=core_recv.at[j, 0],
                device_id={"row": mate}, device_id_type=MESH),
            pltpu.make_async_remote_copy(
                src_ref=zacc.at[j, :, z_part], dst_ref=zcore.at[j],
                send_sem=core_send.at[j, 1], recv_sem=core_recv.at[j, 1],
                device_id={"row": mate}, device_id_type=MESH),
        ]

    def x_copies(j, part):
        found = []
        for d in range(1, nx):
            if part == 0:
                width = pl.ds(0, gram_width(j))
                source, target = gmine.at[j, :, width], gx.at[d - 1, j, :, width]
            else:
                source, target = zmine.at[j], zx.at[d - 1, j]
            found.append(pltpu.make_async_remote_copy(
                src_ref=source, dst_ref=target,
                send_sem=x_send.at[d - 1, j, part], recv_sem=x_recv.at[d - 1, j, part],
                device_id={"row": across_x(d)}, device_id_type=MESH))
        return found

    def back_copies(j, part):
        found = []
        for panel in range(PANELS):
            block = pl.ds(panel * B + j * LANES, LANES)
            if part == 0:
                place = g_ref.at[block, pl.ds(pl.multiple_of(core * B, B), gram_width(j))]
            else:
                place = z_ref.at[block, pl.ds(pl.multiple_of(core * half, half), half)]
            found.append(pltpu.make_async_remote_copy(
                src_ref=place, dst_ref=place,
                send_sem=back_send.at[j, part, panel], recv_sem=back_recv.at[j, part, panel],
                device_id={"row": mate}, device_id_type=MESH))
        return found

    def back_arrive(j, part):
        for panel in range(PANELS):
            block = pl.ds(panel * B + j * LANES, LANES)
            if part == 0:
                place = g_ref.at[block, pl.ds(pl.multiple_of((1 - core) * B, B), gram_width(j))]
            else:
                place = z_ref.at[block, pl.ds(pl.multiple_of((1 - core) * half, half), half)]
            pltpu.make_async_remote_copy(
                src_ref=place, dst_ref=place,
                send_sem=back_send.at[j, part, panel], recv_sem=back_recv.at[j, part, panel],
                device_id={"row": mate}, device_id_type=MESH).wait_recv()

    def core_sum(j):
        z_part = pl.ds(pl.multiple_of(core * half, half), half)
        g_part = pl.ds(pl.multiple_of(core * B, B), gram_width(j))
        first, second = core_copies(j)
        first.wait_recv()
        gmine[j, :, 0:gram_width(j)] = gacc[j, :, g_part] + gcore[j, :, 0:gram_width(j)]
        for copy in x_copies(j, 0):
            copy.start()
        second.wait_recv()
        zmine[j] = zacc[j, :, z_part] + zcore[j]
        for copy in x_copies(j, 1):
            copy.start()

    def x_sum(j, part):
        for copy in x_copies(j, part):
            copy.wait_recv()
        if part == 0:
            summed = gmine[j, :, 0:gram_width(j)]
            for d in range(nx - 1):
                summed = summed + gx[d, j, :, 0:gram_width(j)]
            for panel in range(PANELS):
                g_ref[panel * B + j * LANES:panel * B + (j + 1) * LANES,
                      pl.ds(pl.multiple_of(core * B, B), gram_width(j))] = summed[rows_of(panel)]
        else:
            for panel in range(PANELS):
                summed = zmine[j, rows_of(panel)]
                for d in range(nx - 1):
                    summed = summed + zx[d, j, rows_of(panel)]
                z_ref[panel * B + j * LANES:panel * B + (j + 1) * LANES,
                      pl.ds(pl.multiple_of(core * half, half), half)] = summed
        for copy in back_copies(j, part):
            copy.start()

    zacc[...] = jnp.zeros_like(zacc)
    gacc[...] = jnp.zeros_like(gacc)
    g_ref[...] = jnp.zeros_like(g_ref)
    for t in range(AHEAD):
        relay(t)
    load.wait()
    for j in range(CHUNKS):
        def step(i, carry, j=j):
            t = j * PIECES + GROUP * i
            here = pl.ds(i * GROUP * depth, GROUP * depth)

            @pl.when(t + AHEAD < total)
            def _():
                relay(t + AHEAD)
            for u in range(GROUP):
                arrive(t + u)
            fresh = jnp.concatenate(
                [w_ref[panel * CHUNKS + j, here, :] for panel in range(PANELS)], axis=1)
            turned = fresh.T
            left = split(turned)
            span = cols // GROUP
            for u in range(GROUP):
                if u > 0:
                    @pl.when(t + AHEAD + u < total)
                    def _():
                        relay(t + AHEAD + u)
                for k in range(u * span, (u + 1) * span, 512):
                    right = split(a_ref[here, k:k + 512])
                    zacc[j, :, k:k + 512] += split_dot(left, right, ROWS_COLS)
            for q in range(j + 1):
                old = fresh if q == j else jnp.concatenate(
                    [w_ref[panel * CHUNKS + q, here, :] for panel in range(PANELS)], axis=1)
                gram = exact_dot(turned, old, ROWS_COLS)
                for panel in range(PANELS):
                    spot = panel * B + q * LANES
                    gacc[j, :, spot:spot + LANES] += gram[:, rows_of(panel)]
            if j > 0:
                @pl.when(i == 1)
                def _():
                    core_sum(j - 1)
            return carry
        lax.fori_loop(0, PIECES // GROUP, step, 0)
        for copy in core_copies(j):
            copy.start()
    last = CHUNKS - 1
    core_sum(last)
    for j in range(CHUNKS):
        x_sum(j, 0)
    for j in range(CHUNKS):
        back_arrive(j, 0)
    for j in range(last):
        x_sum(j, 1)
    factor(g_ref, s_ref, m_ref)
    inv_ref[...] = s_ref[:, WIDTH:]
    x_sum(last, 1)

    def waits(t, carry):
        for panel in range(PANELS):
            @pl.when(yy == panel)
            def _():
                @pl.when(zz < nz - 1)
                def _():
                    z_copy(panel, t).wait_send()
                for d in range(1, ny):
                    y_copy(panel, t, d).wait_send()
        return carry
    lax.fori_loop(0, total, waits, 0)
    for j in range(CHUNKS):
        for copy in core_copies(j):
            copy.wait_send()
        for part in range(2):
            for copy in x_copies(j, part):
                copy.wait_send()
            for copy in back_copies(j, part):
                copy.wait_send()
    for j in range(CHUNKS):
        back_arrive(j, 1)


def invert_factor(m_ref):
    lane = lax.broadcasted_iota(jnp.int32, (SUB, LANES), 1)
    sub = lax.broadcasted_iota(jnp.int32, (SUB, LANES), 0)
    strip = m_ref[0:SUB, :]
    for g in range(LANES // SUB):
        base = g * SUB
        left, right = strip[:, :LANES], strip[:, LANES:]
        entry = {}
        for k in range(SUB):
            column = jnp.broadcast_to(left[:, base + k:base + k + 1], (SUB, LANES))
            for i in range(k, SUB):
                entry[i, k] = jnp.broadcast_to(column[i:i + 1, :], (SUB, LANES))
        low, inv = {}, {}
        for k in range(SUB):
            pivot = entry[k, k]
            guess = lax.rsqrt(pivot)
            guess = guess * (1.5 - (0.5 * pivot) * guess * guess)
            inv[k, k] = guess
            for i in range(k + 1, SUB):
                low[i, k] = entry[i, k] * guess
            for j in range(k + 1, SUB):
                for i in range(j, SUB):
                    entry[i, j] = entry[i, j] - low[i, k] * low[j, k]
        for i in range(SUB):
            for j in range(i):
                acc = low[i, j] * inv[j, j]
                for k in range(j + 1, i):
                    acc = acc + low[i, k] * inv[k, j]
                inv[i, j] = -acc * inv[i, i]
        done = []
        for side in (left, right):
            acc = None
            for j in range(SUB):
                weight = jnp.zeros((SUB, LANES), F32)
                for i in range(j, SUB):
                    weight = jnp.where(sub == i, inv[i, j], weight)
                term = weight * side[j:j + 1, :]
                acc = term if acc is None else acc + term
            done.append(acc)
        m_ref[base:base + SUB, :LANES] = done[0]
        m_ref[base:base + SUB, LANES:] = done[1]
        after = base + SUB
        if after < LANES:
            fresh = [m_ref[after:after + SUB, :LANES], m_ref[after:after + SUB, LANES:]]
            for i in range(SUB):
                column = jnp.broadcast_to(done[0][:, after + i:after + i + 1], (SUB, LANES))
                for side in range(2):
                    change = jnp.sum(column * done[side], axis=0, keepdims=True)
                    fresh[side] = jnp.where(sub == i, fresh[side] - change, fresh[side])
            strip = jnp.concatenate(fresh, axis=1)
        if after + SUB < LANES:
            ahead = jnp.where(lane >= after + SUB, done[0], 0.0)
            change = exact_dot(ahead, jnp.concatenate(done, axis=1), ROWS_ROWS)
            m_ref[after + SUB:, :] -= change[after + SUB:, :]


def factor(g_ref, s_ref, m_ref):
    def tile(i, j):
        return g_ref[i * LANES:(i + 1) * LANES, j * LANES:(j + 1) * LANES]

    for i in range(BLOCKS):
        for j in range(BLOCKS):
            known = j % CHUNKS <= i % CHUNKS
            s_ref[i * LANES:(i + 1) * LANES, j * LANES:(j + 1) * LANES] = (
                tile(i, j) if known else tile(j, i).T)
    ident = (lax.broadcasted_iota(jnp.int32, (WIDTH, WIDTH), 0)
             == lax.broadcasted_iota(jnp.int32, (WIDTH, WIDTH), 1)).astype(F32)
    s_ref[:, WIDTH:] = ident
    block_of = lax.broadcasted_iota(jnp.int32, (LANES, WIDTH), 1) // LANES

    def eliminate(b, carry):
        here = pl.ds(pl.multiple_of(b * LANES, LANES), LANES)
        m_ref[:, :LANES] = s_ref[here, here]
        m_ref[:, LANES:] = ident[:LANES, :LANES]
        invert_factor(m_ref)
        strip = exact_dot(m_ref[:, LANES:], s_ref[here, :], ROWS_COLS)
        s_ref[here, :] = strip

        @pl.when(b + 1 < BLOCKS)
        def _():
            ahead = jnp.where(block_of > b, strip[:, :WIDTH], 0.0)
            s_ref[...] -= exact_dot(ahead, strip, ROWS_ROWS)
        return carry
    lax.fori_loop(0, BLOCKS, eliminate, 0)


def update_kernel(scale, inv_ref, z_ref, w_ref, a_ref, r_ref, q_ref, t_ref,
                  inv_high, inv_low, r_high, r_low):
    cols = a_ref.shape[1]

    @pl.when(pl.program_id(0) == 0)
    def _():
        inverse = split(inv_ref[...])
        inv_high[...] = inverse[0]
        inv_low[...] = inverse[1]
        for k in range(0, cols, 512):
            r = split_dot(inverse, split(z_ref[:, k:k + 512]), ROWS_COLS)
            r_ref[:, k:k + 512] = r
            high, low = split(r)
            r_high[:, k:k + 512] = high
            r_low[:, k:k + 512] = low

    w = jnp.concatenate([w_ref[i] for i in range(BLOCKS)], axis=1)
    q = split_dot(split(w), (inv_high[...], inv_low[...]), COLS_COLS)
    q_ref[...] = q * scale
    q = split(q)
    for k in range(0, cols, 512):
        r = r_high[:, k:k + 512], r_low[:, k:k + 512]
        t_ref[:, k:k + 512] = a_ref[:, k:k + 512] - split_dot(q, r, ROWS_COLS)


def on_device(n_row, n_col, matrix):
    rows, cols = matrix.shape
    nx = n_row // 2
    half = cols // 2
    vmem = pl.BlockSpec(memory_space=pltpu.VMEM)
    dma = pltpu.SemaphoreType.DMA
    total = CHUNKS * PIECES
    ny = 1
    while 4 * ny * ny <= n_col:
        ny *= 2
    stacked = PANELS * LANES
    w, z, inverse = pl.pallas_call(
        functools.partial(gather_kernel, n_row, n_col),
        out_shape=(
            jax.ShapeDtypeStruct((BLOCKS, rows, LANES), F32),
            jax.ShapeDtypeStruct((WIDTH, cols), F32),
            jax.ShapeDtypeStruct((WIDTH, WIDTH), F32),
        ),
        in_specs=[pl.BlockSpec(memory_space=pl.ANY)],
        out_specs=(vmem, vmem, vmem),
        scratch_shapes=[
            pltpu.VMEM((rows, cols), F32),
            dma,
            dma((CHUNKS,)),
            pltpu.VMEM((WIDTH, WIDTH), F32),
            pltpu.VMEM((WIDTH, 2 * WIDTH), F32),
            pltpu.VMEM((LANES, 2 * LANES), F32),
            pltpu.VMEM((CHUNKS, stacked, cols), F32),
            pltpu.VMEM((CHUNKS, stacked, WIDTH), F32),
            pltpu.VMEM((CHUNKS, stacked, half), F32),
            pltpu.VMEM((CHUNKS, stacked, B), F32),
            pltpu.VMEM((CHUNKS, stacked, half), F32),
            pltpu.VMEM((CHUNKS, stacked, B), F32),
            pltpu.VMEM((nx - 1, CHUNKS, stacked, half), F32),
            pltpu.VMEM((nx - 1, CHUNKS, stacked, B), F32),
            dma((PANELS, total)),
            dma((total,)),
            dma((ny - 1, total)),
            dma((CHUNKS, 2)),
            dma((CHUNKS, 2)),
            dma((nx - 1, CHUNKS, 2)),
            dma((nx - 1, CHUNKS, 2)),
            dma((CHUNKS, 2, PANELS)),
            dma((CHUNKS, 2, PANELS)),
        ],
        compiler_params=pltpu.CompilerParams(
            collective_id=0, has_side_effects=True, vmem_limit_bytes=60 * 1024 * 1024),
        name="gather_and_multiply",
    )(matrix)
    step = 256
    return pl.pallas_call(
        functools.partial(update_kernel, math.sqrt(rows * n_row)),
        grid=(rows // step,),
        out_shape=(
            jax.ShapeDtypeStruct((WIDTH, cols), F32),
            jax.ShapeDtypeStruct((rows, WIDTH), F32),
            jax.ShapeDtypeStruct((rows, cols), F32),
        ),
        in_specs=[
            vmem,
            vmem,
            pl.BlockSpec((BLOCKS, step, LANES), lambda i: (0, i, 0)),
            pl.BlockSpec((step, cols), lambda i: (i, 0)),
        ],
        out_specs=(
            pl.BlockSpec((WIDTH, cols), lambda i: (0, 0)),
            pl.BlockSpec((step, WIDTH), lambda i: (i, 0)),
            pl.BlockSpec((step, cols), lambda i: (i, 0)),
        ),
        scratch_shapes=[
            pltpu.VMEM((WIDTH, WIDTH), jnp.bfloat16),
            pltpu.VMEM((WIDTH, WIDTH), jnp.bfloat16),
            pltpu.VMEM((WIDTH, cols), jnp.bfloat16),
            pltpu.VMEM((WIDTH, cols), jnp.bfloat16),
        ],
        compiler_params=pltpu.CompilerParams(vmem_limit_bytes=60 * 1024 * 1024),
        name="factor_and_update",
    )(inverse, z, w, matrix)


def solution(mesh):
    sizes = mesh.shape
    placed = (P("row", "col"),)
    return jax.shard_map(
        functools.partial(on_device, sizes["row"], sizes["col"]),
        mesh=mesh,
        in_specs=placed,
        out_specs=(P(None, "col"), P("row", None), P("row", "col")),
        check_vma=False,
    )
```

```python
import functools
import math

import jax
import jax.numpy as jnp
from jax import lax
from jax.experimental import pallas as pl
from jax.experimental.pallas import tpu as pltpu
from jax.sharding import PartitionSpec as P

B = 256
PANELS = 2
LANES = 128
SUB = 8
PIECES = 16
GROUP = 2
AHEAD = 3
PARTS = 4
CHUNKS = B // LANES
BLOCKS = PANELS * CHUNKS
WIDTH = PANELS * B
MESH = pl.DeviceIdType.MESH
F32 = jnp.float32
ROWS_ROWS = (((0,), (0,)), ((), ()))
ROWS_COLS = (((1,), (0,)), ((), ()))
COLS_COLS = (((1,), (1,)), ((), ()))


def exact_dot(left, right, dims):
    return lax.dot_general(
        left, right, dims, precision=lax.Precision.HIGHEST, preferred_element_type=F32
    )


def split(x):
    high = x.astype(jnp.bfloat16)
    return high, (x - high.astype(F32)).astype(jnp.bfloat16)


def split_dot(left, right, dims):
    dot = functools.partial(lax.dot_general, dimension_numbers=dims, preferred_element_type=F32)
    return dot(left[0], right[0]) + (dot(left[0], right[1]) + dot(left[1], right[0]))


def gather_kernel(n_row, n_col, a_hbm, w_ref, z_ref, inv_ref, a_ref, a_sem, p_sem, first_ref, own_gram, mate_gram,
                  pair_gram, x_gram, own_send, own_recv, first_z, first_y, first_recv, g_ref, s_ref, m_ref, zacc, gacc, zcore, gcore, zmine, gmine,
                  zx, gx, piece_recv, z_send, y_send, core_send, core_recv, x_send, x_recv,
                  back_send, back_recv):
    ny = 1
    while 4 * ny * ny <= n_col:
        ny *= 2
    nz = n_col // ny
    nx = n_row // 2
    row, col = lax.axis_index("row"), lax.axis_index("col")
    zz, yy = col // ny, lax.rem(col, ny)
    xx, core = row // 2, lax.rem(row, 2)
    mate = xx * 2 + 1 - core
    rows, cols = a_hbm.shape
    depth = rows // PIECES
    half = cols // 2
    total = CHUNKS * PIECES

    def across_y(d):
        return zz * ny + lax.rem(yy + d, ny)

    def across_x(d):
        return lax.rem(xx + d, nx) * 2 + core

    def panel_copies(panel):
        return [pltpu.make_async_copy(a_hbm.at[:, pl.ds(j * LANES, LANES)],
                                      w_ref.at[panel * CHUNKS + j], p_sem.at[j])
                for j in range(CHUNKS)]

    for panel in range(PANELS):
        @pl.when(col == panel)
        def _():
            for copy in panel_copies(panel):
                copy.start()
    load = pltpu.make_async_copy(a_hbm, a_ref, a_sem)
    load.start()

    barrier = pltpu.get_barrier_semaphore()
    greeted = 0
    for d in sorted({1, nz - 1}):
        pl.semaphore_signal(barrier, inc=1, device_id={"col": lax.rem(zz + d, nz) * ny + yy},
                            device_id_type=MESH)
        greeted += 1
    for d in range(1, ny):
        pl.semaphore_signal(barrier, inc=1, device_id={"col": across_y(d)}, device_id_type=MESH)
        greeted += 1
    for d in range(1, nx):
        pl.semaphore_signal(barrier, inc=1, device_id={"row": across_x(d)}, device_id_type=MESH)
        greeted += 1
    pl.semaphore_signal(barrier, inc=1, device_id={"row": mate}, device_id_type=MESH)
    greeted += 1
    pl.semaphore_wait(barrier, greeted)

    def piece(panel, t):
        return w_ref.at[panel * CHUNKS + t // PIECES, pl.ds(lax.rem(t, PIECES) * depth, depth), :]

    def z_copy(panel, t):
        place = piece(panel, t)
        return pltpu.make_async_remote_copy(
            src_ref=place, dst_ref=place, send_sem=z_send.at[t], recv_sem=piece_recv.at[panel, t],
            device_id={"col": col + ny}, device_id_type=MESH)

    def y_copy(panel, t, d):
        place = piece(panel, t)
        return pltpu.make_async_remote_copy(
            src_ref=place, dst_ref=place, send_sem=y_send.at[d - 1, t],
            recv_sem=piece_recv.at[panel, t],
            device_id={"col": across_y(d)}, device_id_type=MESH)

    def pass_on(panel, t):
        @pl.when(zz < nz - 1)
        def _():
            z_copy(panel, t).start()
        for d in range(1, ny):
            y_copy(panel, t, d).start()

    for panel in range(PANELS):
        @pl.when(col == panel)
        def _():
            def begin(t, carry):
                pass_on(panel, t)
                return carry
            for j, copy in enumerate(panel_copies(panel)):
                copy.wait()
                lax.fori_loop(j * PIECES, (j + 1) * PIECES, begin, 0)

    def relay(t):
        for panel in range(PANELS):
            @pl.when((yy == panel) & (zz > 0))
            def _():
                z_copy(panel, t).wait_recv()
                pass_on(panel, t)

    def arrive(t):
        for panel in range(PANELS):
            @pl.when(yy != panel)
            def _():
                y_copy(panel, t, 1).wait_recv()

    def rows_of(panel):
        return slice(panel * LANES, (panel + 1) * LANES)

    def gram_width(j):
        return (j + 1) * LANES

    def core_copies(j):
        other = 1 - core
        z_part = pl.ds(pl.multiple_of(other * half, half), half)
        g_part = pl.ds(pl.multiple_of(other * B, B), gram_width(j))
        return [
            pltpu.make_async_remote_copy(
                src_ref=gacc.at[j, :, g_part], dst_ref=gcore.at[j, :, pl.ds(0, gram_width(j))],
                send_sem=core_send.at[j, 0], recv_sem=core_recv.at[j, 0],
                device_id={"row": mate}, device_id_type=MESH),
            pltpu.make_async_remote_copy(
                src_ref=zacc.at[j, :, z_part], dst_ref=zcore.at[j],
                send_sem=core_send.at[j, 1], recv_sem=core_recv.at[j, 1],
                device_id={"row": mate}, device_id_type=MESH),
        ]

    def x_copies(j, part):
        found = []
        for d in range(1, nx):
            if part == 0:
                width = pl.ds(0, gram_width(j))
                source, target = gmine.at[j, :, width], gx.at[d - 1, j, :, width]
            else:
                source, target = zmine.at[j], zx.at[d - 1, j]
            found.append(pltpu.make_async_remote_copy(
                src_ref=source, dst_ref=target,
                send_sem=x_send.at[d - 1, j, part], recv_sem=x_recv.at[d - 1, j, part],
                device_id={"row": across_x(d)}, device_id_type=MESH))
        return found

    def back_copies(j, part):
        found = []
        for panel in range(PANELS):
            block = pl.ds(panel * B + j * LANES, LANES)
            if part == 0:
                place = g_ref.at[block, pl.ds(pl.multiple_of(core * B, B), gram_width(j))]
            else:
                place = z_ref.at[block, pl.ds(pl.multiple_of(core * half, half), half)]
            found.append(pltpu.make_async_remote_copy(
                src_ref=place, dst_ref=place,
                send_sem=back_send.at[j, part, panel], recv_sem=back_recv.at[j, part, panel],
                device_id={"row": mate}, device_id_type=MESH))
        return found

    def back_arrive(j, part):
        for panel in range(PANELS):
            block = pl.ds(panel * B + j * LANES, LANES)
            if part == 0:
                place = g_ref.at[block, pl.ds(pl.multiple_of((1 - core) * B, B), gram_width(j))]
            else:
                place = z_ref.at[block, pl.ds(pl.multiple_of((1 - core) * half, half), half)]
            pltpu.make_async_remote_copy(
                src_ref=place, dst_ref=place,
                send_sem=back_send.at[j, part, panel], recv_sem=back_recv.at[j, part, panel],
                device_id={"row": mate}, device_id_type=MESH).wait_recv()

    def core_sum(j):
        z_part = pl.ds(pl.multiple_of(core * half, half), half)
        g_part = pl.ds(pl.multiple_of(core * B, B), gram_width(j))
        first, second = core_copies(j)
        first.wait_recv()
        gmine[j, :, 0:gram_width(j)] = gacc[j, :, g_part] + gcore[j, :, 0:gram_width(j)]
        for copy in x_copies(j, 0):
            copy.start()
        second.wait_recv()
        zmine[j] = zacc[j, :, z_part] + zcore[j]
        for copy in x_copies(j, 1):
            copy.start()

    def x_sum(j, part):
        for copy in x_copies(j, part):
            copy.wait_recv()
        if part == 0:
            summed = gmine[j, :, 0:gram_width(j)]
            for d in range(nx - 1):
                summed = summed + gx[d, j, :, 0:gram_width(j)]
            for panel in range(PANELS):
                g_ref[panel * B + j * LANES:panel * B + (j + 1) * LANES,
                      pl.ds(pl.multiple_of(core * B, B), gram_width(j))] = summed[rows_of(panel)]
        else:
            for panel in range(PANELS):
                summed = zmine[j, rows_of(panel)]
                for d in range(nx - 1):
                    summed = summed + zx[d, j, rows_of(panel)]
                z_ref[panel * B + j * LANES:panel * B + (j + 1) * LANES,
                      pl.ds(pl.multiple_of(core * half, half), half)] = summed
        for copy in back_copies(j, part):
            copy.start()

    def own_copies():
        found = [pltpu.make_async_remote_copy(
            src_ref=own_gram, dst_ref=mate_gram, send_sem=own_send.at[0], recv_sem=own_recv.at[0],
            device_id={"row": mate}, device_id_type=MESH)]
        for d in range(1, nx):
            found.append(pltpu.make_async_remote_copy(
                src_ref=pair_gram, dst_ref=x_gram.at[d - 1],
                send_sem=own_send.at[d], recv_sem=own_recv.at[d],
                device_id={"row": across_x(d)}, device_id_type=MESH))
        return found

    def first_z_copy(k):
        place = first_ref.at[pl.ds(k * (B // PARTS), B // PARTS), :]
        return pltpu.make_async_remote_copy(
            src_ref=place, dst_ref=place, send_sem=first_z.at[k], recv_sem=first_recv.at[k],
            device_id={"col": col + ny}, device_id_type=MESH)

    def first_y_copy(k, d):
        place = first_ref.at[pl.ds(k * (B // PARTS), B // PARTS), :]
        return pltpu.make_async_remote_copy(
            src_ref=place, dst_ref=place, send_sem=first_y.at[d - 1, k],
            recv_sem=first_recv.at[k],
            device_id={"col": across_y(d)}, device_id_type=MESH)

    def first_on(k):
        @pl.when(zz < nz - 1)
        def _():
            first_z_copy(k).start()
        for d in range(1, ny):
            first_y_copy(k, d).start()

    @pl.when(col == 0)
    def _():
        own_gram[...] = jnp.zeros_like(own_gram)

        def add(i, carry):
            here = pl.ds(i * B, B)
            part = jnp.concatenate([w_ref[j, here, :] for j in range(CHUNKS)], axis=1)
            own_gram[...] += exact_dot(part.T, part, ROWS_COLS)
            return carry
        lax.fori_loop(0, rows // B, add, 0)
        copies = own_copies()
        copies[0].start()
        copies[0].wait_recv()
        pair_gram[...] = own_gram[...] + mate_gram[...]
        for copy in copies[1:]:
            copy.start()
        for copy in copies[1:]:
            copy.wait_recv()
        summed = pair_gram[...]
        for d in range(nx - 1):
            summed = summed + x_gram[d]
        s_ref[:, :WIDTH] = identity()
        s_ref[:, WIDTH:] = identity()
        s_ref[0:B, 0:B] = summed
        eliminate(s_ref, m_ref, 0, CHUNKS)
        first_ref[...] = s_ref[0:B, WIDTH:WIDTH + B]
        for k in range(PARTS):
            first_on(k)
        for copy in copies:
            copy.wait_send()

    zacc[...] = jnp.zeros_like(zacc)
    gacc[...] = jnp.zeros_like(gacc)
    g_ref[...] = jnp.zeros_like(g_ref)
    for t in range(AHEAD):
        relay(t)
    load.wait()
    for j in range(CHUNKS):
        def step(i, carry, j=j):
            t = j * PIECES + GROUP * i
            here = pl.ds(i * GROUP * depth, GROUP * depth)

            @pl.when(t + AHEAD < total)
            def _():
                relay(t + AHEAD)
            for u in range(GROUP):
                arrive(t + u)
            fresh = jnp.concatenate(
                [w_ref[panel * CHUNKS + j, here, :] for panel in range(PANELS)], axis=1)
            turned = fresh.T
            left = split(turned)
            span = cols // GROUP
            for u in range(GROUP):
                if u > 0:
                    @pl.when(t + AHEAD + u < total)
                    def _():
                        relay(t + AHEAD + u)
                for k in range(u * span, (u + 1) * span, 512):
                    right = split(a_ref[here, k:k + 512])
                    zacc[j, :, k:k + 512] += split_dot(left, right, ROWS_COLS)
            for q in range(j + 1):
                old = fresh if q == j else jnp.concatenate(
                    [w_ref[panel * CHUNKS + q, here, :] for panel in range(PANELS)], axis=1)
                gram = exact_dot(turned, old, ROWS_COLS)
                for panel in range(PANELS):
                    spot = panel * B + q * LANES
                    gacc[j, :, spot:spot + LANES] += gram[:, rows_of(panel)]
            if j > 0:
                @pl.when(i == 1)
                def _():
                    core_sum(j - 1)
            return carry
        lax.fori_loop(0, PIECES // GROUP, step, 0)
        for copy in core_copies(j):
            copy.start()
    last = CHUNKS - 1
    core_sum(last)
    for k in range(PARTS):
        @pl.when((yy == 0) & (zz > 0))
        def _(k=k):
            first_z_copy(k).wait_recv()
            first_on(k)

        @pl.when(yy != 0)
        def _(k=k):
            first_y_copy(k, 1).wait_recv()
    for j in range(CHUNKS):
        x_sum(j, 0)
    for j in range(CHUNKS):
        back_arrive(j, 0)
    for j in range(last):
        x_sum(j, 1)
    factor(g_ref, first_ref, s_ref, m_ref)
    inv_ref[...] = s_ref[:, WIDTH:]
    x_sum(last, 1)

    def waits(t, carry):
        for panel in range(PANELS):
            @pl.when(yy == panel)
            def _():
                @pl.when(zz < nz - 1)
                def _():
                    z_copy(panel, t).wait_send()
                for d in range(1, ny):
                    y_copy(panel, t, d).wait_send()
        return carry
    lax.fori_loop(0, total, waits, 0)

    @pl.when(yy == 0)
    def _():
        for k in range(PARTS):
            @pl.when(zz < nz - 1)
            def _(k=k):
                first_z_copy(k).wait_send()
            for d in range(1, ny):
                first_y_copy(k, d).wait_send()
    for j in range(CHUNKS):
        for copy in core_copies(j):
            copy.wait_send()
        for part in range(2):
            for copy in x_copies(j, part):
                copy.wait_send()
            for copy in back_copies(j, part):
                copy.wait_send()
    for j in range(CHUNKS):
        back_arrive(j, 1)


def invert_factor(m_ref):
    lane = lax.broadcasted_iota(jnp.int32, (SUB, LANES), 1)
    sub = lax.broadcasted_iota(jnp.int32, (SUB, LANES), 0)
    strip = m_ref[0:SUB, :]
    for g in range(LANES // SUB):
        base = g * SUB
        left, right = strip[:, :LANES], strip[:, LANES:]
        entry = {}
        for k in range(SUB):
            column = jnp.broadcast_to(left[:, base + k:base + k + 1], (SUB, LANES))
            for i in range(k, SUB):
                entry[i, k] = jnp.broadcast_to(column[i:i + 1, :], (SUB, LANES))
        low, inv = {}, {}
        for k in range(SUB):
            pivot = entry[k, k]
            guess = lax.rsqrt(pivot)
            guess = guess * (1.5 - (0.5 * pivot) * guess * guess)
            inv[k, k] = guess
            for i in range(k + 1, SUB):
                low[i, k] = entry[i, k] * guess
            for j in range(k + 1, SUB):
                for i in range(j, SUB):
                    entry[i, j] = entry[i, j] - low[i, k] * low[j, k]
        for i in range(SUB):
            for j in range(i):
                acc = low[i, j] * inv[j, j]
                for k in range(j + 1, i):
                    acc = acc + low[i, k] * inv[k, j]
                inv[i, j] = -acc * inv[i, i]
        done = []
        for side in (left, right):
            acc = None
            for j in range(SUB):
                weight = jnp.zeros((SUB, LANES), F32)
                for i in range(j, SUB):
                    weight = jnp.where(sub == i, inv[i, j], weight)
                term = weight * side[j:j + 1, :]
                acc = term if acc is None else acc + term
            done.append(acc)
        m_ref[base:base + SUB, :LANES] = done[0]
        m_ref[base:base + SUB, LANES:] = done[1]
        after = base + SUB
        if after < LANES:
            fresh = [m_ref[after:after + SUB, :LANES], m_ref[after:after + SUB, LANES:]]
            for i in range(SUB):
                column = jnp.broadcast_to(done[0][:, after + i:after + i + 1], (SUB, LANES))
                for side in range(2):
                    change = jnp.sum(column * done[side], axis=0, keepdims=True)
                    fresh[side] = jnp.where(sub == i, fresh[side] - change, fresh[side])
            strip = jnp.concatenate(fresh, axis=1)
        if after + SUB < LANES:
            ahead = jnp.where(lane >= after + SUB, done[0], 0.0)
            change = exact_dot(ahead, jnp.concatenate(done, axis=1), ROWS_ROWS)
            m_ref[after + SUB:, :] -= change[after + SUB:, :]


def identity():
    return (lax.broadcasted_iota(jnp.int32, (WIDTH, WIDTH), 0)
            == lax.broadcasted_iota(jnp.int32, (WIDTH, WIDTH), 1)).astype(F32)


def eliminate(s_ref, m_ref, start, stop):
    block_of = lax.broadcasted_iota(jnp.int32, (LANES, WIDTH), 1) // LANES

    def one(b, carry):
        here = pl.ds(pl.multiple_of(b * LANES, LANES), LANES)
        m_ref[:, :LANES] = s_ref[here, here]
        m_ref[:, LANES:] = identity()[:LANES, :LANES]
        invert_factor(m_ref)
        strip = exact_dot(m_ref[:, LANES:], s_ref[here, :], ROWS_COLS)
        s_ref[here, :] = strip

        @pl.when(b + 1 < stop)
        def _():
            ahead = jnp.where(block_of > b, strip[:, :WIDTH], 0.0)
            s_ref[...] -= exact_dot(ahead, strip, ROWS_ROWS)
        return carry
    lax.fori_loop(start, stop, one, 0)


def factor(g_ref, first_ref, s_ref, m_ref):
    def tile(i, j):
        return g_ref[i * LANES:(i + 1) * LANES, j * LANES:(j + 1) * LANES]

    for i in range(BLOCKS):
        for j in range(BLOCKS):
            known = j % CHUNKS <= i % CHUNKS
            s_ref[i * LANES:(i + 1) * LANES, j * LANES:(j + 1) * LANES] = (
                tile(i, j) if known else tile(j, i).T)
    s_ref[:, WIDTH:] = identity()
    strip = exact_dot(first_ref[...], s_ref[0:B, :], ROWS_COLS)
    s_ref[0:B, :] = strip
    s_ref[B:WIDTH, :] -= exact_dot(strip[:, B:WIDTH], strip, ROWS_ROWS)
    eliminate(s_ref, m_ref, CHUNKS, BLOCKS)


def update_kernel(scale, inv_ref, z_ref, w_ref, a_ref, r_ref, q_ref, t_ref,
                  inv_high, inv_low, r_high, r_low):
    cols = a_ref.shape[1]

    @pl.when(pl.program_id(0) == 0)
    def _():
        inverse = split(inv_ref[...])
        inv_high[...] = inverse[0]
        inv_low[...] = inverse[1]
        for k in range(0, cols, 512):
            r = split_dot(inverse, split(z_ref[:, k:k + 512]), ROWS_COLS)
            r_ref[:, k:k + 512] = r
            high, low = split(r)
            r_high[:, k:k + 512] = high
            r_low[:, k:k + 512] = low

    w = jnp.concatenate([w_ref[i] for i in range(BLOCKS)], axis=1)
    q = split_dot(split(w), (inv_high[...], inv_low[...]), COLS_COLS)
    q_ref[...] = q * scale
    q = split(q)
    for k in range(0, cols, 512):
        r = r_high[:, k:k + 512], r_low[:, k:k + 512]
        t_ref[:, k:k + 512] = a_ref[:, k:k + 512] - split_dot(q, r, ROWS_COLS)


def on_device(n_row, n_col, matrix):
    rows, cols = matrix.shape
    nx = n_row // 2
    half = cols // 2
    vmem = pl.BlockSpec(memory_space=pltpu.VMEM)
    dma = pltpu.SemaphoreType.DMA
    total = CHUNKS * PIECES
    ny = 1
    while 4 * ny * ny <= n_col:
        ny *= 2
    stacked = PANELS * LANES
    w, z, inverse = pl.pallas_call(
        functools.partial(gather_kernel, n_row, n_col),
        out_shape=(
            jax.ShapeDtypeStruct((BLOCKS, rows, LANES), F32),
            jax.ShapeDtypeStruct((WIDTH, cols), F32),
            jax.ShapeDtypeStruct((WIDTH, WIDTH), F32),
        ),
        in_specs=[pl.BlockSpec(memory_space=pl.ANY)],
        out_specs=(vmem, vmem, vmem),
        scratch_shapes=[
            pltpu.VMEM((rows, cols), F32),
            dma,
            dma((CHUNKS,)),
            pltpu.VMEM((B, B), F32),
            pltpu.VMEM((B, B), F32),
            pltpu.VMEM((B, B), F32),
            pltpu.VMEM((B, B), F32),
            pltpu.VMEM((nx - 1, B, B), F32),
            dma((nx,)),
            dma((nx,)),
            dma((PARTS,)),
            dma((ny - 1, PARTS)),
            dma((PARTS,)),
            pltpu.VMEM((WIDTH, WIDTH), F32),
            pltpu.VMEM((WIDTH, 2 * WIDTH), F32),
            pltpu.VMEM((LANES, 2 * LANES), F32),
            pltpu.VMEM((CHUNKS, stacked, cols), F32),
            pltpu.VMEM((CHUNKS, stacked, WIDTH), F32),
            pltpu.VMEM((CHUNKS, stacked, half), F32),
            pltpu.VMEM((CHUNKS, stacked, B), F32),
            pltpu.VMEM((CHUNKS, stacked, half), F32),
            pltpu.VMEM((CHUNKS, stacked, B), F32),
            pltpu.VMEM((nx - 1, CHUNKS, stacked, half), F32),
            pltpu.VMEM((nx - 1, CHUNKS, stacked, B), F32),
            dma((PANELS, total)),
            dma((total,)),
            dma((ny - 1, total)),
            dma((CHUNKS, 2)),
            dma((CHUNKS, 2)),
            dma((nx - 1, CHUNKS, 2)),
            dma((nx - 1, CHUNKS, 2)),
            dma((CHUNKS, 2, PANELS)),
            dma((CHUNKS, 2, PANELS)),
        ],
        compiler_params=pltpu.CompilerParams(
            collective_id=0, has_side_effects=True, vmem_limit_bytes=60 * 1024 * 1024),
        name="gather_and_multiply",
    )(matrix)
    step = 256
    return pl.pallas_call(
        functools.partial(update_kernel, math.sqrt(rows * n_row)),
        grid=(rows // step,),
        out_shape=(
            jax.ShapeDtypeStruct((WIDTH, cols), F32),
            jax.ShapeDtypeStruct((rows, WIDTH), F32),
            jax.ShapeDtypeStruct((rows, cols), F32),
        ),
        in_specs=[
            vmem,
            vmem,
            pl.BlockSpec((BLOCKS, step, LANES), lambda i: (0, i, 0)),
            pl.BlockSpec((step, cols), lambda i: (i, 0)),
        ],
        out_specs=(
            pl.BlockSpec((WIDTH, cols), lambda i: (0, 0)),
            pl.BlockSpec((step, WIDTH), lambda i: (i, 0)),
            pl.BlockSpec((step, cols), lambda i: (i, 0)),
        ),
        scratch_shapes=[
            pltpu.VMEM((WIDTH, WIDTH), jnp.bfloat16),
            pltpu.VMEM((WIDTH, WIDTH), jnp.bfloat16),
            pltpu.VMEM((WIDTH, cols), jnp.bfloat16),
            pltpu.VMEM((WIDTH, cols), jnp.bfloat16),
        ],
        compiler_params=pltpu.CompilerParams(vmem_limit_bytes=60 * 1024 * 1024),
        name="factor_and_update",
    )(inverse, z, w, matrix)


def solution(mesh):
    sizes = mesh.shape
    placed = (P("row", "col"),)
    return jax.shard_map(
        functools.partial(on_device, sizes["row"], sizes["col"]),
        mesh=mesh,
        in_specs=placed,
        out_specs=(P(None, "col"), P("row", None), P("row", "col")),
        check_vma=False,
    )
```

```python
import functools
import math

import jax
import jax.numpy as jnp
from jax import lax
from jax.experimental import pallas as pl
from jax.experimental.pallas import tpu as pltpu
from jax.sharding import PartitionSpec as P

B = 256
PANELS = 2
LANES = 128
SUB = 8
PIECES = 16
GROUP = 2
AHEAD = 3
PARTS = 4
CHUNKS = B // LANES
BLOCKS = PANELS * CHUNKS
WIDTH = PANELS * B
MESH = pl.DeviceIdType.MESH
F32 = jnp.float32
ROWS_ROWS = (((0,), (0,)), ((), ()))
ROWS_COLS = (((1,), (0,)), ((), ()))
COLS_COLS = (((1,), (1,)), ((), ()))


def exact_dot(left, right, dims):
    return lax.dot_general(
        left, right, dims, precision=lax.Precision.HIGHEST, preferred_element_type=F32
    )


def split(x):
    high = x.astype(jnp.bfloat16)
    return high, (x - high.astype(F32)).astype(jnp.bfloat16)


def split_dot(left, right, dims):
    dot = functools.partial(lax.dot_general, dimension_numbers=dims, preferred_element_type=F32)
    return dot(left[0], right[0]) + (dot(left[0], right[1]) + dot(left[1], right[0]))


def gather_kernel(n_row, n_col, a_hbm, w_ref, z_ref, inv_ref, a_ref, a_sem, p_sem, first_ref, own_gram, mate_gram,
                  pair_gram, x_gram, own_send, own_recv, first_z, first_y, first_recv, g_ref, s_ref, m_ref, zacc, gacc, zcore, gcore, zmine, gmine,
                  zx, gx, piece_recv, z_send, y_send, core_send, core_recv, x_send, x_recv,
                  back_send, back_recv):
    ny = 1
    while 4 * ny * ny <= n_col:
        ny *= 2
    nz = n_col // ny
    nx = n_row // 2
    row, col = lax.axis_index("row"), lax.axis_index("col")
    zz, yy = col // ny, lax.rem(col, ny)
    xx, core = row // 2, lax.rem(row, 2)
    mate = xx * 2 + 1 - core
    rows, cols = a_hbm.shape
    depth = rows // PIECES
    half = cols // 2
    total = CHUNKS * PIECES

    def across_y(d):
        return zz * ny + lax.rem(yy + d, ny)

    def across_x(d):
        return lax.rem(xx + d, nx) * 2 + core

    def panel_copies(panel):
        return [pltpu.make_async_copy(a_hbm.at[:, pl.ds(j * LANES, LANES)],
                                      w_ref.at[panel * CHUNKS + j], p_sem.at[j])
                for j in range(CHUNKS)]

    for panel in range(PANELS):
        @pl.when(col == panel)
        def _():
            for copy in panel_copies(panel):
                copy.start()
    load = pltpu.make_async_copy(a_hbm, a_ref, a_sem)
    load.start()

    barrier = pltpu.get_barrier_semaphore()
    greeted = 0
    for d in sorted({1, nz - 1}):
        pl.semaphore_signal(barrier, inc=1, device_id={"col": lax.rem(zz + d, nz) * ny + yy},
                            device_id_type=MESH)
        greeted += 1
    for d in range(1, ny):
        pl.semaphore_signal(barrier, inc=1, device_id={"col": across_y(d)}, device_id_type=MESH)
        greeted += 1
    for d in range(1, nx):
        pl.semaphore_signal(barrier, inc=1, device_id={"row": across_x(d)}, device_id_type=MESH)
        greeted += 1
    pl.semaphore_signal(barrier, inc=1, device_id={"row": mate}, device_id_type=MESH)
    greeted += 1
    pl.semaphore_wait(barrier, greeted)

    def piece(panel, t):
        return w_ref.at[panel * CHUNKS + t // PIECES, pl.ds(lax.rem(t, PIECES) * depth, depth), :]

    def z_copy(panel, t):
        place = piece(panel, t)
        return pltpu.make_async_remote_copy(
            src_ref=place, dst_ref=place, send_sem=z_send.at[t], recv_sem=piece_recv.at[panel, t],
            device_id={"col": col + ny}, device_id_type=MESH)

    def y_copy(panel, t, d):
        place = piece(panel, t)
        return pltpu.make_async_remote_copy(
            src_ref=place, dst_ref=place, send_sem=y_send.at[d - 1, t],
            recv_sem=piece_recv.at[panel, t],
            device_id={"col": across_y(d)}, device_id_type=MESH)

    def pass_on(panel, t):
        @pl.when(zz < nz - 1)
        def _():
            z_copy(panel, t).start()
        for d in range(1, ny):
            y_copy(panel, t, d).start()

    for panel in range(PANELS):
        @pl.when(col == panel)
        def _():
            def begin(t, carry):
                pass_on(panel, t)
                return carry
            for j, copy in enumerate(panel_copies(panel)):
                copy.wait()
                lax.fori_loop(j * PIECES, (j + 1) * PIECES, begin, 0)

    def relay(t):
        for panel in range(PANELS):
            @pl.when((yy == panel) & (zz > 0))
            def _():
                z_copy(panel, t).wait_recv()
                pass_on(panel, t)

    def arrive(t):
        for panel in range(PANELS):
            @pl.when(yy != panel)
            def _():
                y_copy(panel, t, 1).wait_recv()

    def rows_of(panel):
        return slice(panel * LANES, (panel + 1) * LANES)

    def gram_width(j):
        return (j + 1) * LANES

    def core_copies(j):
        other = 1 - core
        z_part = pl.ds(pl.multiple_of(other * half, half), half)
        g_part = pl.ds(pl.multiple_of(other * B, B), gram_width(j))
        return [
            pltpu.make_async_remote_copy(
                src_ref=gacc.at[j, :, g_part], dst_ref=gcore.at[j, :, pl.ds(0, gram_width(j))],
                send_sem=core_send.at[j, 0], recv_sem=core_recv.at[j, 0],
                device_id={"row": mate}, device_id_type=MESH),
            pltpu.make_async_remote_copy(
                src_ref=zacc.at[j, :, z_part], dst_ref=zcore.at[j],
                send_sem=core_send.at[j, 1], recv_sem=core_recv.at[j, 1],
                device_id={"row": mate}, device_id_type=MESH),
        ]

    def x_copies(j, part):
        found = []
        for d in range(1, nx):
            if part == 0:
                width = pl.ds(0, gram_width(j))
                source, target = gmine.at[j, :, width], gx.at[d - 1, j, :, width]
            else:
                source, target = zmine.at[j], zx.at[d - 1, j]
            found.append(pltpu.make_async_remote_copy(
                src_ref=source, dst_ref=target,
                send_sem=x_send.at[d - 1, j, part], recv_sem=x_recv.at[d - 1, j, part],
                device_id={"row": across_x(d)}, device_id_type=MESH))
        return found

    def back_copies(j, part):
        found = []
        for panel in range(PANELS):
            block = pl.ds(panel * B + j * LANES, LANES)
            if part == 0:
                place = g_ref.at[block, pl.ds(pl.multiple_of(core * B, B), gram_width(j))]
            else:
                place = z_ref.at[block, pl.ds(pl.multiple_of(core * half, half), half)]
            found.append(pltpu.make_async_remote_copy(
                src_ref=place, dst_ref=place,
                send_sem=back_send.at[j, part, panel], recv_sem=back_recv.at[j, part, panel],
                device_id={"row": mate}, device_id_type=MESH))
        return found

    def back_arrive(j, part):
        for panel in range(PANELS):
            block = pl.ds(panel * B + j * LANES, LANES)
            if part == 0:
                place = g_ref.at[block, pl.ds(pl.multiple_of((1 - core) * B, B), gram_width(j))]
            else:
                place = z_ref.at[block, pl.ds(pl.multiple_of((1 - core) * half, half), half)]
            pltpu.make_async_remote_copy(
                src_ref=place, dst_ref=place,
                send_sem=back_send.at[j, part, panel], recv_sem=back_recv.at[j, part, panel],
                device_id={"row": mate}, device_id_type=MESH).wait_recv()

    def core_sum(j):
        z_part = pl.ds(pl.multiple_of(core * half, half), half)
        g_part = pl.ds(pl.multiple_of(core * B, B), gram_width(j))
        first, second = core_copies(j)
        first.wait_recv()
        gmine[j, :, 0:gram_width(j)] = gacc[j, :, g_part] + gcore[j, :, 0:gram_width(j)]
        for copy in x_copies(j, 0):
            copy.start()
        second.wait_recv()
        zmine[j] = zacc[j, :, z_part] + zcore[j]
        for copy in x_copies(j, 1):
            copy.start()

    def x_sum(j, part):
        for copy in x_copies(j, part):
            copy.wait_recv()
        if part == 0:
            summed = gmine[j, :, 0:gram_width(j)]
            for d in range(nx - 1):
                summed = summed + gx[d, j, :, 0:gram_width(j)]
            for panel in range(PANELS):
                g_ref[panel * B + j * LANES:panel * B + (j + 1) * LANES,
                      pl.ds(pl.multiple_of(core * B, B), gram_width(j))] = summed[rows_of(panel)]
        else:
            for panel in range(PANELS):
                summed = zmine[j, rows_of(panel)]
                for d in range(nx - 1):
                    summed = summed + zx[d, j, rows_of(panel)]
                z_ref[panel * B + j * LANES:panel * B + (j + 1) * LANES,
                      pl.ds(pl.multiple_of(core * half, half), half)] = summed
        for copy in back_copies(j, part):
            copy.start()

    def own_copies():
        found = [pltpu.make_async_remote_copy(
            src_ref=own_gram, dst_ref=mate_gram, send_sem=own_send.at[0], recv_sem=own_recv.at[0],
            device_id={"row": mate}, device_id_type=MESH)]
        for d in range(1, nx):
            found.append(pltpu.make_async_remote_copy(
                src_ref=pair_gram, dst_ref=x_gram.at[d - 1],
                send_sem=own_send.at[d], recv_sem=own_recv.at[d],
                device_id={"row": across_x(d)}, device_id_type=MESH))
        return found

    def first_z_copy(k):
        place = first_ref.at[pl.ds(k * (B // PARTS), B // PARTS), :]
        return pltpu.make_async_remote_copy(
            src_ref=place, dst_ref=place, send_sem=first_z.at[k], recv_sem=first_recv.at[k],
            device_id={"col": col + ny}, device_id_type=MESH)

    def first_y_copy(k, d):
        place = first_ref.at[pl.ds(k * (B // PARTS), B // PARTS), :]
        return pltpu.make_async_remote_copy(
            src_ref=place, dst_ref=place, send_sem=first_y.at[d - 1, k],
            recv_sem=first_recv.at[k],
            device_id={"col": across_y(d)}, device_id_type=MESH)

    def first_on(k):
        @pl.when(zz < nz - 1)
        def _():
            first_z_copy(k).start()
        for d in range(1, ny):
            first_y_copy(k, d).start()

    @pl.when(col == 0)
    def _():
        own_gram[...] = jnp.zeros_like(own_gram)

        def add(i, carry):
            here = pl.ds(i * B, B)
            part = jnp.concatenate([w_ref[j, here, :] for j in range(CHUNKS)], axis=1)
            own_gram[...] += exact_dot(part.T, part, ROWS_COLS)
            return carry
        lax.fori_loop(0, rows // B, add, 0)
        copies = own_copies()
        copies[0].start()
        copies[0].wait_recv()
        pair_gram[...] = own_gram[...] + mate_gram[...]
        for copy in copies[1:]:
            copy.start()
        for copy in copies[1:]:
            copy.wait_recv()
        summed = pair_gram[...]
        for d in range(nx - 1):
            summed = summed + x_gram[d]
        s_ref[:, :WIDTH] = identity()
        s_ref[:, WIDTH:] = identity()
        s_ref[0:B, 0:B] = summed
        eliminate(s_ref, m_ref, 0, CHUNKS)
        first_ref[...] = s_ref[0:B, WIDTH:WIDTH + B]
        for k in range(PARTS):
            first_on(k)
        for copy in copies:
            copy.wait_send()

    zacc[...] = jnp.zeros_like(zacc)
    gacc[...] = jnp.zeros_like(gacc)
    g_ref[...] = jnp.zeros_like(g_ref)
    for t in range(AHEAD):
        relay(t)
    load.wait()
    for j in range(CHUNKS):
        def step(i, carry, j=j):
            t = j * PIECES + GROUP * i
            here = pl.ds(i * GROUP * depth, GROUP * depth)

            @pl.when(t + AHEAD < total)
            def _():
                relay(t + AHEAD)
            for u in range(GROUP):
                arrive(t + u)
            fresh = jnp.concatenate(
                [w_ref[panel * CHUNKS + j, here, :] for panel in range(PANELS)], axis=1)
            turned = fresh.T
            left = split(turned)
            span = cols // GROUP
            for u in range(GROUP):
                if u > 0:
                    @pl.when(t + AHEAD + u < total)
                    def _():
                        relay(t + AHEAD + u)
                for k in range(u * span, (u + 1) * span, 512):
                    right = split(a_ref[here, k:k + 512])
                    zacc[j, :, k:k + 512] += split_dot(left, right, ROWS_COLS)
            for q in range(j + 1):
                old = fresh if q == j else jnp.concatenate(
                    [w_ref[panel * CHUNKS + q, here, :] for panel in range(PANELS)], axis=1)
                gram = exact_dot(turned, old, ROWS_COLS)
                for panel in range(PANELS):
                    spot = panel * B + q * LANES
                    gacc[j, :, spot:spot + LANES] += gram[:, rows_of(panel)]
            if j > 0:
                @pl.when(i == 1)
                def _():
                    core_sum(j - 1)
            return carry
        lax.fori_loop(0, PIECES // GROUP, step, 0)
        for copy in core_copies(j):
            copy.start()
    last = CHUNKS - 1
    core_sum(last)
    for k in range(PARTS):
        @pl.when((yy == 0) & (zz > 0))
        def _(k=k):
            first_z_copy(k).wait_recv()
            first_on(k)

        @pl.when(yy != 0)
        def _(k=k):
            first_y_copy(k, 1).wait_recv()
    for j in range(CHUNKS):
        x_sum(j, 0)
    for j in range(CHUNKS):
        back_arrive(j, 0)
    for j in range(last):
        x_sum(j, 1)
    factor(g_ref, first_ref, s_ref, m_ref)
    inv_ref[...] = s_ref[:, WIDTH:]
    x_sum(last, 1)

    def waits(t, carry):
        for panel in range(PANELS):
            @pl.when(yy == panel)
            def _():
                @pl.when(zz < nz - 1)
                def _():
                    z_copy(panel, t).wait_send()
                for d in range(1, ny):
                    y_copy(panel, t, d).wait_send()
        return carry
    lax.fori_loop(0, total, waits, 0)

    @pl.when(yy == 0)
    def _():
        for k in range(PARTS):
            @pl.when(zz < nz - 1)
            def _(k=k):
                first_z_copy(k).wait_send()
            for d in range(1, ny):
                first_y_copy(k, d).wait_send()
    for j in range(CHUNKS):
        for copy in core_copies(j):
            copy.wait_send()
        for part in range(2):
            for copy in x_copies(j, part):
                copy.wait_send()
            for copy in back_copies(j, part):
                copy.wait_send()
    for j in range(CHUNKS):
        back_arrive(j, 1)


def invert_factor(m_ref):
    lane = lax.broadcasted_iota(jnp.int32, (SUB, LANES), 1)
    sub = lax.broadcasted_iota(jnp.int32, (SUB, LANES), 0)
    strip = m_ref[0:SUB, :]
    for g in range(LANES // SUB):
        base = g * SUB
        left, right = strip[:, :LANES], strip[:, LANES:]
        entry = {}
        for k in range(SUB):
            column = jnp.broadcast_to(left[:, base + k:base + k + 1], (SUB, LANES))
            for i in range(k, SUB):
                entry[i, k] = jnp.broadcast_to(column[i:i + 1, :], (SUB, LANES))
        low, inv = {}, {}
        for k in range(SUB):
            pivot = entry[k, k]
            guess = lax.rsqrt(pivot)
            guess = guess * (1.5 - (0.5 * pivot) * guess * guess)
            inv[k, k] = guess
            for i in range(k + 1, SUB):
                low[i, k] = entry[i, k] * guess
            for j in range(k + 1, SUB):
                for i in range(j, SUB):
                    entry[i, j] = entry[i, j] - low[i, k] * low[j, k]
        for i in range(SUB):
            for j in range(i):
                acc = low[i, j] * inv[j, j]
                for k in range(j + 1, i):
                    acc = acc + low[i, k] * inv[k, j]
                inv[i, j] = -acc * inv[i, i]
        done = []
        for side in (left, right):
            acc = None
            for j in range(SUB):
                weight = jnp.zeros((SUB, LANES), F32)
                for i in range(j, SUB):
                    weight = jnp.where(sub == i, inv[i, j], weight)
                term = weight * side[j:j + 1, :]
                acc = term if acc is None else acc + term
            done.append(acc)
        m_ref[base:base + SUB, :LANES] = done[0]
        m_ref[base:base + SUB, LANES:] = done[1]
        after = base + SUB
        if after < LANES:
            fresh = [m_ref[after:after + SUB, :LANES], m_ref[after:after + SUB, LANES:]]
            for i in range(SUB):
                column = jnp.broadcast_to(done[0][:, after + i:after + i + 1], (SUB, LANES))
                for side in range(2):
                    change = jnp.sum(column * done[side], axis=0, keepdims=True)
                    fresh[side] = jnp.where(sub == i, fresh[side] - change, fresh[side])
            strip = jnp.concatenate(fresh, axis=1)
        if after + SUB < LANES:
            ahead = jnp.where(lane >= after + SUB, done[0], 0.0)
            change = exact_dot(ahead, jnp.concatenate(done, axis=1), ROWS_ROWS)
            m_ref[after + SUB:, :] -= change[after + SUB:, :]


def identity():
    return (lax.broadcasted_iota(jnp.int32, (WIDTH, WIDTH), 0)
            == lax.broadcasted_iota(jnp.int32, (WIDTH, WIDTH), 1)).astype(F32)


def eliminate(s_ref, m_ref, start, stop):
    block_of = lax.broadcasted_iota(jnp.int32, (LANES, WIDTH), 1) // LANES

    def one(b, carry):
        here = pl.ds(pl.multiple_of(b * LANES, LANES), LANES)
        m_ref[:, :LANES] = s_ref[here, here]
        m_ref[:, LANES:] = identity()[:LANES, :LANES]
        invert_factor(m_ref)
        strip = exact_dot(m_ref[:, LANES:], s_ref[here, :], ROWS_COLS)
        s_ref[here, :] = strip

        @pl.when(b + 1 < stop)
        def _():
            ahead = jnp.where(block_of > b, strip[:, :WIDTH], 0.0)
            s_ref[...] -= exact_dot(ahead, strip, ROWS_ROWS)
        return carry
    lax.fori_loop(start, stop, one, 0)


def factor(g_ref, first_ref, s_ref, m_ref):
    def tile(i, j):
        return g_ref[i * LANES:(i + 1) * LANES, j * LANES:(j + 1) * LANES]

    for i in range(BLOCKS):
        for j in range(BLOCKS):
            known = j % CHUNKS <= i % CHUNKS
            s_ref[i * LANES:(i + 1) * LANES, j * LANES:(j + 1) * LANES] = (
                tile(i, j) if known else tile(j, i).T)
    s_ref[:, WIDTH:] = identity()
    strip = exact_dot(first_ref[...], s_ref[0:B, :], ROWS_COLS)
    s_ref[0:B, :] = strip
    s_ref[B:WIDTH, :] -= exact_dot(strip[:, B:WIDTH], strip, ROWS_ROWS)
    eliminate(s_ref, m_ref, CHUNKS, BLOCKS)


def update_kernel(scale, inv_ref, z_ref, w_ref, a_ref, r_ref, q_ref, t_ref,
                  inv_high, inv_low, r_high, r_low):
    cols = a_ref.shape[1]

    @pl.when(pl.program_id(0) == 0)
    def _():
        inverse = split(inv_ref[...])
        inv_high[...] = inverse[0]
        inv_low[...] = inverse[1]
        for k in range(0, cols, 512):
            r = split_dot(inverse, split(z_ref[:, k:k + 512]), ROWS_COLS)
            r_ref[:, k:k + 512] = r
            high, low = split(r)
            r_high[:, k:k + 512] = high
            r_low[:, k:k + 512] = low

    w = jnp.concatenate([w_ref[i] for i in range(BLOCKS)], axis=1)
    q = split_dot(split(w), (inv_high[...], inv_low[...]), COLS_COLS)
    q_ref[...] = q * scale
    q = split(q)
    for k in range(0, cols, 512):
        r = r_high[:, k:k + 512], r_low[:, k:k + 512]
        t_ref[:, k:k + 512] = a_ref[:, k:k + 512] - split_dot(q, r, ROWS_COLS)


def on_device(n_row, n_col, matrix):
    rows, cols = matrix.shape
    nx = n_row // 2
    half = cols // 2
    vmem = pl.BlockSpec(memory_space=pltpu.VMEM)
    dma = pltpu.SemaphoreType.DMA
    total = CHUNKS * PIECES
    ny = 1
    while 4 * ny * ny <= n_col:
        ny *= 2
    stacked = PANELS * LANES
    w, z, inverse = pl.pallas_call(
        functools.partial(gather_kernel, n_row, n_col),
        out_shape=(
            jax.ShapeDtypeStruct((BLOCKS, rows, LANES), F32),
            jax.ShapeDtypeStruct((WIDTH, cols), F32),
            jax.ShapeDtypeStruct((WIDTH, WIDTH), F32),
        ),
        in_specs=[pl.BlockSpec(memory_space=pl.ANY)],
        out_specs=(vmem, vmem, vmem),
        scratch_shapes=[
            pltpu.VMEM((rows, cols), F32),
            dma,
            dma((CHUNKS,)),
            pltpu.VMEM((B, B), F32),
            pltpu.VMEM((B, B), F32),
            pltpu.VMEM((B, B), F32),
            pltpu.VMEM((B, B), F32),
            pltpu.VMEM((nx - 1, B, B), F32),
            dma((nx,)),
            dma((nx,)),
            dma((PARTS,)),
            dma((ny - 1, PARTS)),
            dma((PARTS,)),
            pltpu.VMEM((WIDTH, WIDTH), F32),
            pltpu.VMEM((WIDTH, 2 * WIDTH), F32),
            pltpu.VMEM((LANES, 2 * LANES), F32),
            pltpu.VMEM((CHUNKS, stacked, cols), F32),
            pltpu.VMEM((CHUNKS, stacked, WIDTH), F32),
            pltpu.VMEM((CHUNKS, stacked, half), F32),
            pltpu.VMEM((CHUNKS, stacked, B), F32),
            pltpu.VMEM((CHUNKS, stacked, half), F32),
            pltpu.VMEM((CHUNKS, stacked, B), F32),
            pltpu.VMEM((nx - 1, CHUNKS, stacked, half), F32),
            pltpu.VMEM((nx - 1, CHUNKS, stacked, B), F32),
            dma((PANELS, total)),
            dma((total,)),
            dma((ny - 1, total)),
            dma((CHUNKS, 2)),
            dma((CHUNKS, 2)),
            dma((nx - 1, CHUNKS, 2)),
            dma((nx - 1, CHUNKS, 2)),
            dma((CHUNKS, 2, PANELS)),
            dma((CHUNKS, 2, PANELS)),
        ],
        compiler_params=pltpu.CompilerParams(
            collective_id=0, has_side_effects=True, vmem_limit_bytes=60 * 1024 * 1024),
        name="gather_and_multiply",
    )(matrix)
    step = 512
    return pl.pallas_call(
        functools.partial(update_kernel, math.sqrt(rows * n_row)),
        grid=(rows // step,),
        out_shape=(
            jax.ShapeDtypeStruct((WIDTH, cols), F32),
            jax.ShapeDtypeStruct((rows, WIDTH), F32),
            jax.ShapeDtypeStruct((rows, cols), F32),
        ),
        in_specs=[
            vmem,
            vmem,
            pl.BlockSpec((BLOCKS, step, LANES), lambda i: (0, i, 0)),
            pl.BlockSpec((step, cols), lambda i: (i, 0)),
        ],
        out_specs=(
            pl.BlockSpec((WIDTH, cols), lambda i: (0, 0)),
            pl.BlockSpec((step, WIDTH), lambda i: (i, 0)),
            pl.BlockSpec((step, cols), lambda i: (i, 0)),
        ),
        scratch_shapes=[
            pltpu.VMEM((WIDTH, WIDTH), jnp.bfloat16),
            pltpu.VMEM((WIDTH, WIDTH), jnp.bfloat16),
            pltpu.VMEM((WIDTH, cols), jnp.bfloat16),
            pltpu.VMEM((WIDTH, cols), jnp.bfloat16),
        ],
        compiler_params=pltpu.CompilerParams(vmem_limit_bytes=60 * 1024 * 1024),
        name="factor_and_update",
    )(inverse, z, w, matrix)


def solution(mesh):
    sizes = mesh.shape
    placed = (P("row", "col"),)
    return jax.shard_map(
        functools.partial(on_device, sizes["row"], sizes["col"]),
        mesh=mesh,
        in_specs=placed,
        out_specs=(P(None, "col"), P("row", None), P("row", "col")),
        check_vma=False,
    )
```
